512 devices in a mesh: member: 4 (over x_lo, core), region: 128 (over z, y, x_hi).
Axes of the slice: x: 4 (x_hi: 2, x_lo: 2; x = x_hi * 2 + x_lo), y: 8, z: 8, core: 2. Of those that a mesh axis runs over, the one named last changes fastest.
Arguments:
- prior_tracer_ensemble: float32 [80, 1024, 2048], P('member', 'region'), may hold values from -6 to 6
- diffusion_numbers: float32 [1024, 2048], P('region'), may hold values from 0.02 to 0.24
- measured_site_index: int32 [4, 2048], P(None, 'region'), may hold values from 0 to 16383
- measured_readings: float32 [4, 2048], P(None, 'region'), may hold values from -6 to 6
- measurement_error_spread: float32 [4, 2048], P(None, 'region'), may hold values from 0.1 to 1
- measured_slot_tally: int32 [4, 128], replicated, may hold values from 1 to 16, 1024 in all within a row
Outputs:
- analysis: float32 [80, 1024, 2048], P(None, 'region', 'member')
The draws below stay inside these ranges and needn't reach their ends.
Inputs may be any that keep to these rules, and one draw needn't show every extreme that they name: `measured_slot_tally`: the live slots of a region are its first ones; the counts of each batch sum to 8 times the number of regions and reach 16 in some region.
All inputs are finite; a program needn't handle non-finite values.
Results may differ from the reference program's by a relative error of at most 0.0003.
Values sent between devices are 32-bit elements; how exact they have to be, the bound alone decides.
No kernel may reach another device: no remote copies, remote signals or barrier semaphores. Data moves between devices by JAX's collectives and lax.ppermute only.
A program may use at most 64 MiB of HBM per device.

```python
import math
import jax
import jax.numpy as jnp
import numpy as np
from jax import lax

ENSEMBLE_SIZE = 80
CX = 8
MESH_WIDTH = 2048
OBS_REG = 8
REACH = 2
NB = 4
REGIONS = 128
CAP = 16
SLOTS = 2048
RADIUS = 16
MESH_HEIGHT = 1024
N_REGION = 128


def touch_ends(drawn, stream_key, least, largest):
    extent = drawn.shape
    place = [jax.random.randint(jax.random.fold_in(stream_key, axis), (), 0, extent[axis]) for axis in range(len(extent))]
    drawn = drawn.at[tuple(place)].set(least)
    longest = extent.index(max(extent))
    place[longest] = (place[longest] + 1) % extent[longest]
    return drawn.at[tuple(place)].set(largest)


def level_of(key, shape, shards, smallest, top_value):
    def one(dim, shards_of):
        draws = jax.random.uniform(jax.random.fold_in(jax.random.fold_in(key, 6), dim), (shards_of,), jnp.float32, smallest / len(shards), top_value / len(shards))
        return jnp.repeat(jnp.exp(draws), shape[dim] // shards_of).reshape((-1,) + (1,) * (len(shape) - dim - 1))

    level = one(*shards[0])
    for cut in shards[1:]:
        level = level * one(*cut)
    return level


def profile(number_of, total, reach, slope):
    weights = [(1 << 20) // math.isqrt(grade ** slope) + 1 for grade in range(2, number_of + 1)]
    surplus, holding = total - reach - (number_of - 1), [1] * (number_of - 1)
    while surplus > 0:
        movable = [i for i in range(number_of - 1) if holding[i] < reach]
        mass, budget = sum([weights[i] for i in movable]), surplus
        for i in movable:
            more = min(reach - holding[i], max(1, budget * weights[i] // mass), surplus)
            holding[i] = holding[i] + more
            surplus = surplus - more
    return np.array([reach] + holding)


def uneven_parts(key, amount, total, most, lean):
    if amount == 2:
        one = jax.random.randint(key, (), max(1, total - most), min(most, total - 1) + 1)
        return jnp.stack([one, total - one])
    sizes = jnp.asarray(profile(amount, total, most, lean), jnp.int32)
    couples = (amount - 1) // 2
    giver, receiver = sizes[1:1 + 2 * couples:2], sizes[2:2 + 2 * couples:2]
    room = jnp.minimum(giver - 1, most - receiver)
    moved = jax.random.randint(jax.random.fold_in(key, 1), (couples,), 0, 1 << 20) % (room + 1)
    sizes = sizes.at[1:1 + 2 * couples:2].set(giver - moved).at[2:2 + 2 * couples:2].set(receiver + moved)
    return sizes[jax.random.permutation(jax.random.fold_in(key, 2), amount)]


def noise(rng, dims, scale, limit, pieces=(), held_as=jnp.bfloat16):
    result = scale * jax.random.normal(rng, dims, jnp.float32)
    if pieces:
        result = result * level_of(rng, dims, pieces, -0.22, 0.18)
    return jnp.clip(result, -limit, limit).astype(held_as)


def setup_inputs(seed: int = 0) -> dict:
    splits = jax.random.split(jax.random.key(seed), 7)
    return {
        "prior_tracer_ensemble": noise(splits[0], (ENSEMBLE_SIZE, MESH_HEIGHT, MESH_WIDTH), 1.0, 6.0, ((0, 4), (1, 128)), jnp.float32),
        "diffusion_numbers": jnp.clip(jnp.exp(math.log(0.24) - 2.4849066 * jax.random.uniform(splits[1], (MESH_HEIGHT, MESH_WIDTH), jnp.float32) ** level_of(splits[1], (MESH_HEIGHT, MESH_WIDTH), ((0, 128),), -0.2, 0.2)), 0.02, 0.24),
        "measured_site_index": touch_ends(jax.random.randint(splits[2], (NB, SLOTS), 0, CX * MESH_WIDTH), jax.random.fold_in(splits[2], 1), 0, (CX * MESH_WIDTH) - 1).astype(jnp.int32),
        "measured_readings": noise(splits[3], (NB, SLOTS), 1.5, 6.0, ((1, 128),), jnp.float32),
        "measurement_error_spread": jnp.clip(jnp.exp(math.log(1.0) - 2.3025851 * jax.random.uniform(splits[4], (NB, SLOTS), jnp.float32) ** level_of(splits[4], (NB, SLOTS), ((1, 128),), -0.2, 0.2)), 0.1, 1.0),
        "measured_slot_tally": jax.vmap(lambda own: uneven_parts(own, REGIONS, OBS_REG * REGIONS, CAP, 2))(jax.random.split(splits[5], NB)).reshape((NB, REGIONS)).astype(jnp.int32),
    }


epsilon = 1e-05
highest = lax.Precision.HIGHEST

def forward_diffuse(prior_tracer_ensemble, diffusion_numbers):
    haloed_tracer = jnp.pad(prior_tracer_ensemble, ((0, 0), (1, 1), (0, 0)))
    lower_boundary_lines = haloed_tracer[:, :-2, :]
    upper_boundary_lines = haloed_tracer[:, 2:, :]
    eastern_strips = jnp.roll(prior_tracer_ensemble, -1, axis=2)
    western_strips = jnp.roll(prior_tracer_ensemble, 1, axis=2)
    return prior_tracer_ensemble + diffusion_numbers[None] * (upper_boundary_lines + lower_boundary_lines + eastern_strips + western_strips - 4.0 * prior_tracer_ensemble)

def increments(obs_prior, measured_readings, measurement_error_spread, live_slots):
    members = obs_prior.shape[1]
    average = lax.optimization_barrier(jnp.mean(obs_prior, axis=1, keepdims=True))
    anomaly = obs_prior - average
    spread = lax.optimization_barrier(jnp.sum(anomaly * anomaly, axis=1, keepdims=True)) / (members - 1) + epsilon
    obs_noise = jnp.where(live_slots > 0.5, measurement_error_spread, 1.0)[:, None]
    posterior = 1.0 / (1.0 / spread + 1.0 / obs_noise)
    post_mean = posterior * (average / spread + measured_readings[:, None] / obs_noise)
    increment = post_mean - average + (jnp.sqrt(posterior / spread) - 1.0) * anomaly
    return (anomaly, spread[:, 0], increment)

def taper_weights(cell_rows, cell_cols, obs_rows, obs_cols, vertical_sums, radius):
    row_gap = cell_rows[:, None] - obs_rows[None, :]
    col_gap = jnp.abs(cell_cols[:, None] - obs_cols[None, :])
    col_gap = jnp.minimum(col_gap, vertical_sums - col_gap)
    scaled_gap = (row_gap * row_gap + col_gap * col_gap) / float(radius * radius)
    remain = jnp.maximum(1.0 - scaled_gap, 0.0)
    return remain * remain

def regress(region_block, anomaly, spread, increment, weights):
    members = region_block.shape[0]
    average = lax.optimization_barrier(jnp.mean(region_block, axis=0, keepdims=True))
    state_anomaly = region_block - average
    covariance = jnp.einsum('ec,je->cj', state_anomaly, anomaly, precision=highest) / (members - 1)
    regression = weights * covariance / spread[None, :]
    return region_block + jnp.einsum('cj,je->ec', regression, increment, precision=highest)

def pad_slots(values, margin):
    widths = ((margin, margin),) + ((0, 0),) * (values.ndim - 1)
    return jnp.pad(values, widths)

def reference(prior_tracer_ensemble, diffusion_numbers, measured_site_index, measured_readings, measurement_error_spread, measured_slot_tally):
    ensemble_tracers = forward_diffuse(prior_tracer_ensemble, diffusion_numbers)
    window = (2 * REACH + 1) * CAP
    margin = REACH * CAP
    slot_index = jnp.arange(SLOTS, dtype=jnp.int32)
    owner_region = slot_index // CAP
    cell_index = jnp.arange(CX * MESH_WIDTH, dtype=jnp.int32)
    for batch_index in range(NB):
        obs_cells = measured_site_index[batch_index]
        local_rows = obs_cells // MESH_WIDTH
        obs_cols = obs_cells % MESH_WIDTH
        obs_rows = owner_region * CX + local_rows
        obs_prior = ensemble_tracers[:, obs_rows, obs_cols].T
        live_slots = (slot_index % CAP < measured_slot_tally[batch_index][owner_region]).astype(jnp.float32)
        wide_prior = pad_slots(obs_prior, margin)
        wide_value = pad_slots(measured_readings[batch_index], margin)
        wide_var = pad_slots(measurement_error_spread[batch_index], margin)
        wide_live = pad_slots(live_slots, margin)
        wide_rows = pad_slots(obs_rows.astype(jnp.float32), margin)
        wide_cols = pad_slots(obs_cols.astype(jnp.float32), margin)
        anomaly, spread, increment = increments(wide_prior, wide_value, wide_var, wide_live)

        def update_region(region_id):
            start = region_id * CAP
            near_anomaly = lax.dynamic_slice_in_dim(anomaly, start, window, 0)
            near_spread = lax.dynamic_slice_in_dim(spread, start, window, 0)
            near_increment = lax.dynamic_slice_in_dim(increment, start, window, 0)
            near_live = lax.dynamic_slice_in_dim(wide_live, start, window, 0)
            near_rows = lax.dynamic_slice_in_dim(wide_rows, start, window, 0)
            near_cols = lax.dynamic_slice_in_dim(wide_cols, start, window, 0)
            region_block = lax.dynamic_slice_in_dim(ensemble_tracers, region_id * CX, CX, 1).reshape(ENSEMBLE_SIZE, CX * MESH_WIDTH)
            cell_rows = (region_id * CX + cell_index // MESH_WIDTH).astype(jnp.float32)
            cell_cols = (cell_index % MESH_WIDTH).astype(jnp.float32)
            weights = taper_weights(cell_rows, cell_cols, near_rows, near_cols, MESH_WIDTH, RADIUS) * near_live[None, :]
            return regress(region_block, near_anomaly, near_spread, near_increment, weights)
        updated = lax.map(update_region, jnp.arange(N_REGION, dtype=jnp.int32))
        ensemble_tracers = updated.reshape(N_REGION, ENSEMBLE_SIZE, CX, MESH_WIDTH).transpose(1, 0, 2, 3).reshape(ENSEMBLE_SIZE, MESH_HEIGHT, MESH_WIDTH)
    return ensemble_tracers
```

```python
import functools

import jax
import jax.numpy as jnp
from jax import lax
from jax.experimental import pallas as pl
from jax.experimental.pallas import tpu as pltpu
from jax.sharding import PartitionSpec as P

REACH = 2
RADIUS = 16
epsilon = 1e-05
LANES = 128
f32 = jnp.float32
bf16 = jnp.bfloat16

FACTS = 5
READING, VARIANCE, ROW, COLUMN, LIVE = range(FACTS)


def lane_of(shape):
    return lax.broadcasted_iota(jnp.int32, shape, len(shape) - 1)


def row_of(shape):
    return lax.broadcasted_iota(jnp.int32, shape, len(shape) - 2)


def halves(x):
    hi = x.astype(bf16).astype(f32)
    return hi, x - hi


def product(a, b, dims):
    a_hi, a_lo = [v.astype(bf16) for v in halves(a)]
    b_hi, b_lo = [v.astype(bf16) for v in halves(b)]
    dot = functools.partial(lax.dot_general, dimension_numbers=(dims, ((), ())), preferred_element_type=f32)
    return dot(a_hi, b_hi) + (dot(a_hi, b_lo) + dot(a_lo, b_hi))


def step_kernel(
    region_ref, site_ref, tally_ref, tracer_ref, above_ref, below_ref, diffusion_ref,
    site_vec_ref, reading_ref, variance_ref, stepped_ref, parcel_ref, board,
):
    own, rows, width = tracer_ref.shape
    batches, slots = site_ref.shape
    copies = parcel_ref.shape[0]
    quarters = 4
    tiles = width // LANES // quarters
    region = region_ref[0]
    diffusion = diffusion_ref[...]
    row = row_of((rows, width))
    for e in range(own):
        x = tracer_ref[e]
        lower = jnp.where(row == 0, above_ref[e : e + 1, :], pltpu.roll(x, 1, 0))
        upper = jnp.where(row == rows - 1, below_ref[e : e + 1, :], pltpu.roll(x, rows - 1, 0))
        east = pltpu.roll(x, width - 1, 1)
        west = pltpu.roll(x, 1, 1)
        y = x + diffusion * (upper + lower + east + west - 4.0 * x)
        for q in range(quarters):
            for t in range(tiles):
                at = ((q * own + e) * tiles + t) * rows
                col = (q * tiles + t) * LANES
                stepped_ref[at : at + rows, :] = y[:, col : col + LANES]
    board[...] = jnp.zeros_like(board)
    lane = lane_of((own, LANES))
    for b in range(batches):
        picked = jnp.zeros((own, LANES), f32)
        for k in range(slots):
            cell = site_ref[b, k]
            col = lax.rem(cell, width)
            tile = lax.div(col, LANES)
            start = lax.div(tile, tiles) * (own * tiles * rows) + lax.rem(tile, tiles) * rows + lax.div(cell, width)
            line = stepped_ref[pl.ds(start, own, stride=tiles * rows), :]
            shift = lax.rem(k - lax.rem(col, LANES) + LANES, LANES)
            picked = jnp.where(lane == k, pltpu.roll(line, shift, 1), picked)
        at = b * 32
        board[at : at + own, :] = picked
        cells = site_vec_ref[b : b + 1, :]
        count = tally_ref[b, region]
        facts = [
            reading_ref[b : b + 1, :],
            variance_ref[b : b + 1, :],
            (region * rows + lax.div(cells, width)).astype(f32),
            lax.rem(cells, width).astype(f32),
            jnp.where(lane_of((1, slots)) < count, 1.0, 0.0),
        ]
        for i, fact in enumerate(facts):
            board[at + own + i : at + own + i + 1, 0:slots] = fact
    parcel = board[...].T[:slots, :]
    for i in range(copies):
        parcel_ref[i] = parcel


def gather_kernel(parcels_ref, pair_ref):
    count, slots, _ = parcels_ref.shape
    members = count // 2
    own = 20
    lane = lane_of((slots, LANES))
    for b in range(4):
        for p in range(2):
            total = jnp.zeros((slots, LANES), f32)
            for m in range(members):
                moved = pltpu.roll(parcels_ref[p * members + m], (own * m - 32 * b) % LANES, 1)
                end = own * (m + 1) + (FACTS if m == members - 1 else 0)
                total = jnp.where((lane >= own * m) & (lane < end), moved, total)
            at = (b * 2 + p) * slots
            pair_ref[at : at + slots, :] = total


def beside(hi, lo):
    lane = lane_of(hi.shape)
    again = pltpu.roll(hi, 80, 1)
    last = pltpu.roll(lo, 32, 1)
    first = jnp.where(lane < 80, hi, again)
    second = jnp.where(lane < 32, again, last)
    return jnp.concatenate([first.astype(bf16), second.astype(bf16)], axis=1)


def below_each_other(x):
    hi, lo = halves(x)
    hi, lo = hi.astype(bf16), lo.astype(bf16)
    return jnp.concatenate([hi, lo, hi, jnp.zeros((16, x.shape[1]), bf16)], axis=0)


def update_kernel(
    place_ref, own_ref, minus_ref, plus_ref, down_ref, up_ref, state_ref,
    out_ref, obs, inc_ref, ano_ref, gain_lhs, inc_lhs, near_ref, board, updated, *, width,
):
    members = 80
    parity = place_ref[0]
    quarter = place_ref[1]
    region = place_ref[2]
    rows, quarter_width = out_ref.shape[1:]
    tiles = quarter_width // LANES
    scale = 1.0 / (RADIUS * RADIUS)
    pieces = [
        (down_ref, 160), (down_ref, 96), (down_ref, 0), (minus_ref, 0), (own_ref, 0), (plus_ref, 0), (up_ref, 0), (up_ref, 96), (up_ref, 160),
        (down_ref, 128), (down_ref, 32), (minus_ref, 32), (own_ref, 32), (plus_ref, 32), (up_ref, 32), (up_ref, 128),
        (down_ref, 64), (minus_ref, 64), (own_ref, 64), (plus_ref, 64), (up_ref, 64),
        (minus_ref, 96), (own_ref, 96), (plus_ref, 96),
    ]
    for i, (ref, at) in enumerate(pieces):
        obs[32 * i : 32 * i + 32, :] = ref[at : at + 32, :]
    starts = [0, 288, 512, 672, 768]
    centres = [96, 64, 32, 0]
    total = starts[-1]
    pick = jnp.where(lane_of((8, LANES)) == members + ROW + row_of((8, LANES)), 1.0, 0.0)
    across = lax.dot_general(
        pick, obs[...], (((1,), (1,)), ((), ())), precision=lax.Precision.HIGHEST, preferred_element_type=f32
    )
    for b in range(4):
        n = starts[b + 1] - starts[b]
        x = obs[starts[b] : starts[b + 1], :]
        member = lane_of((n, LANES)) < members
        fact = lambda i: x[:, members + i : members + i + 1]
        average = jnp.sum(jnp.where(member, x, 0.0), axis=1, keepdims=True) / members
        anomaly = jnp.where(member, x - average, 0.0)
        spread = jnp.sum(anomaly * anomaly, axis=1, keepdims=True) / (members - 1) + epsilon
        live = fact(LIVE)
        noise = jnp.where(live > 0.5, fact(VARIANCE), 1.0)
        posterior = 1.0 / (1.0 / spread + 1.0 / noise)
        post_mean = posterior * (average / spread + fact(READING) / noise)
        increment = post_mean - average + (jnp.sqrt(posterior / spread) - 1.0) * anomaly
        increment = jnp.where(member, increment, 0.0)
        scaled = anomaly * (live / ((members - 1) * spread))
        inc_ref[0:n, :] = increment
        ano_ref[0:n, :] = scaled
        at = centres[b] + 16 * parity
        gain_lhs[b] = beside(*halves(ano_ref[pl.ds(at, 80), :]))
        near_ref[b] = obs[pl.ds(starts[b] + at, 80), :]
        board[...] = jnp.zeros_like(board)
        board[0:80, :] = inc_ref[pl.ds(at, 80), :]
        inc_lhs[b] = beside(*halves(board[...].T[0:80, :]))
        if b < 3:
            y = obs[starts[b + 1] : total, :]
            m = total - starts[b + 1]
            inside = lane_of((m, LANES)) < members
            mean = jnp.sum(jnp.where(inside, y, 0.0), axis=1, keepdims=True) / members
            off = jnp.where(inside, y - mean, 0.0)
            covariance = product(off, scaled, ((1,), (1,)))
            row_gap = y[:, members + ROW : members + ROW + 1] - across[0:1, starts[b] : starts[b + 1]]
            col_gap = jnp.abs(y[:, members + COLUMN : members + COLUMN + 1] - across[1:2, starts[b] : starts[b + 1]])
            col_gap = jnp.minimum(col_gap, width - col_gap)
            remain = jnp.maximum(1.0 - (row_gap * row_gap + col_gap * col_gap) * scale, 0.0)
            weights = remain * remain * covariance
            obs[starts[b + 1] : total, :] = y + product(weights, increment, ((1,), (0,)))
    cols = (lane_of((80, quarter_width)) + quarter * quarter_width).astype(f32)
    closeness = []
    for b in range(4):
        gap = jnp.abs(cols - near_ref[b, :, members + COLUMN : members + COLUMN + 1])
        gap = jnp.minimum(gap, width - gap)
        closeness.append(1.0 - gap * gap * scale)
    for r in range(rows):
        state = jnp.concatenate(
            [state_ref[pl.ds(t * rows + r, members, stride=tiles * rows), :] for t in range(tiles)], axis=1
        )
        for b in range(4):
            mean = jnp.mean(state, axis=0, keepdims=True)
            covariance = jnp.dot(gain_lhs[b], below_each_other(state - mean), preferred_element_type=f32)
            gap = (region * rows + r).astype(f32) - near_ref[b, :, members + ROW : members + ROW + 1]
            remain = jnp.maximum(closeness[b] - gap * gap * scale, 0.0)
            weights = remain * remain * covariance
            state = state + jnp.dot(inc_lhs[b], below_each_other(weights), preferred_element_type=f32)
        for t in range(tiles):
            updated[pl.ds(t * rows + r, members, stride=tiles * rows), :] = state[:, t * LANES : (t + 1) * LANES]
    for e in range(members):
        for t in range(tiles):
            at = (e * tiles + t) * rows
            out_ref[e, :, t * LANES : (t + 1) * LANES] = updated[at : at + rows, :]


def local(tracer, diffusion, sites, readings, variances, tally):
    own, rows, width = tracer.shape
    regions = lax.axis_size("region")
    quarters = lax.axis_size("member")
    batches, slots = sites.shape
    quarter_width = width // quarters
    members = own * quarters
    region = lax.axis_index("region")
    quarter = lax.axis_index("member")
    upward = [(i, i + 1) for i in range(regions - 1)]
    downward = [(i + 1, i) for i in range(regions - 1)]
    above = lax.ppermute(tracer[:, rows - 1, :], "region", upward)
    below = lax.ppermute(tracer[:, 0, :], "region", downward)
    vmem = pl.BlockSpec(memory_space=pltpu.VMEM)
    smem = pl.BlockSpec(memory_space=pltpu.SMEM)
    limit = pltpu.CompilerParams(vmem_limit_bytes=32 * 1024 * 1024)
    stepped, parcel = pl.pallas_call(
        step_kernel,
        out_shape=(
            jax.ShapeDtypeStruct((own * rows * width // LANES, LANES), f32),
            jax.ShapeDtypeStruct((2 * quarters, slots, LANES), f32),
        ),
        in_specs=[smem] * 3 + [vmem] * 7,
        out_specs=(vmem, vmem),
        scratch_shapes=[pltpu.VMEM((LANES, LANES), f32)],
        compiler_params=limit,
        name="step",
    )(region[None].astype(jnp.int32), sites, tally, tracer, above, below, diffusion, sites, readings, variances)
    lines = [[2 * quarters * g + i for i in range(2 * quarters)] for g in range(regions // 2)]
    parcels = lax.all_to_all(parcel, ("region", "member"), 0, 0, axis_index_groups=lines)
    state = lax.all_to_all(
        stepped.reshape(quarters, own * rows * quarter_width // LANES, LANES), "member", 0, 0
    ).reshape(members * rows * quarter_width // LANES, LANES)
    pair = pl.pallas_call(
        gather_kernel,
        out_shape=jax.ShapeDtypeStruct((batches * 2 * slots, LANES), f32),
        in_specs=[vmem],
        out_specs=vmem,
        name="gather",
    )(parcels)

    def shifted(value, steps):
        return lax.ppermute(value, "region", [(i, (i + steps) % regions) for i in range(regions)])

    block = 2 * slots
    minus, plus = shifted(pair, 2), shifted(pair, -2)
    down = shifted(jnp.concatenate([plus[: 3 * block], pair[: 2 * block], minus[:block]]), 6)
    up = shifted(jnp.concatenate([minus[: 3 * block], pair[: 2 * block], plus[:block]]), -6)
    place = jnp.stack([region % 2, quarter, region]).astype(jnp.int32)
    total = 24 * block
    return pl.pallas_call(
        functools.partial(update_kernel, width=width),
        out_shape=jax.ShapeDtypeStruct((members, rows, quarter_width), f32),
        in_specs=[smem] + [vmem] * 6,
        out_specs=vmem,
        scratch_shapes=[
            pltpu.VMEM((total, LANES), f32),
            pltpu.VMEM((9 * block, LANES), f32),
            pltpu.VMEM((9 * block, LANES), f32),
            pltpu.VMEM((4, 80, 256), bf16),
            pltpu.VMEM((4, 80, 256), bf16),
            pltpu.VMEM((4, 80, LANES), f32),
            pltpu.VMEM((LANES, LANES), f32),
            pltpu.VMEM(state.shape, f32),
        ],
        compiler_params=limit,
        name="update",
    )(place, pair, minus, plus, down, up, state)


def solution(mesh):
    placed = (
        P("member", "region", None),
        P("region", None),
        P(None, "region"),
        P(None, "region"),
        P(None, "region"),
        P(),
    )
    return jax.shard_map(
        local, mesh=mesh, in_specs=placed, out_specs=P(None, "region", "member"), check_vma=False
    )
```

```python
import functools

import jax
import jax.numpy as jnp
from jax import lax
from jax.experimental import pallas as pl
from jax.experimental.pallas import tpu as pltpu
from jax.sharding import PartitionSpec as P

REACH = 2
RADIUS = 16
epsilon = 1e-05
LANES = 128
QUARTERS = 4
RING = 8
f32 = jnp.float32
bf16 = jnp.bfloat16

FACTS = 5
READING, VARIANCE, ROW, COLUMN, LIVE = range(FACTS)


def lane_of(shape):
    return lax.broadcasted_iota(jnp.int32, shape, len(shape) - 1)


def row_of(shape):
    return lax.broadcasted_iota(jnp.int32, shape, len(shape) - 2)


def halves(x):
    hi = x.astype(bf16).astype(f32)
    return hi, x - hi


def product(a, b, dims):
    a_hi, a_lo = [v.astype(bf16) for v in halves(a)]
    b_hi, b_lo = [v.astype(bf16) for v in halves(b)]
    dot = functools.partial(lax.dot_general, dimension_numbers=(dims, ((), ())), preferred_element_type=f32)
    return dot(a_hi, b_hi) + (dot(a_hi, b_lo) + dot(a_lo, b_hi))


def edges_kernel(tracer_ref, top_ref, bottom_ref):
    own, rows, _ = tracer_ref.shape
    for e in range(own):
        top_ref[e : e + 1, :] = tracer_ref[e, 0:1, :]
        bottom_ref[e : e + 1, :] = tracer_ref[e, rows - 1 : rows, :]


def step_kernel(
    region_ref, site_ref, tally_ref, tracer_ref, diffusion_ref, site_vec_ref, reading_ref, variance_ref,
    partial_ref, board_ref,
):
    own, rows, width = tracer_ref.shape
    batches, slots = site_ref.shape
    tiles = width // LANES // QUARTERS
    region = region_ref[0]
    diffusion = diffusion_ref[...]
    row = row_of((rows, width))
    for e in range(own):
        x = tracer_ref[e]
        lower = jnp.where(row == 0, 0.0, pltpu.roll(x, 1, 0))
        upper = jnp.where(row == rows - 1, 0.0, pltpu.roll(x, rows - 1, 0))
        east = pltpu.roll(x, width - 1, 1)
        west = pltpu.roll(x, 1, 1)
        y = x + diffusion * (upper + lower + east + west - 4.0 * x)
        for q in range(QUARTERS):
            for t in range(tiles):
                at = ((q * own + e) * tiles + t) * rows
                col = (q * tiles + t) * LANES
                partial_ref[at : at + rows, :] = y[:, col : col + LANES]
    board_ref[...] = jnp.zeros_like(board_ref)
    lane = lane_of((own, LANES))
    for b in range(batches):
        picked = jnp.zeros((own, LANES), f32)
        for k in range(slots):
            cell = site_ref[b, k]
            col = lax.rem(cell, width)
            tile = lax.div(col, LANES)
            start = lax.div(tile, tiles) * (own * tiles * rows) + lax.rem(tile, tiles) * rows + lax.div(cell, width)
            line = partial_ref[pl.ds(start, own, stride=tiles * rows), :]
            shift = lax.rem(k - lax.rem(col, LANES) + LANES, LANES)
            picked = jnp.where(lane == k, pltpu.roll(line, shift, 1), picked)
        at = b * 32
        board_ref[at : at + own, :] = picked
        cells = site_vec_ref[b : b + 1, :]
        count = tally_ref[b, region]
        facts = [
            reading_ref[b : b + 1, :],
            variance_ref[b : b + 1, :],
            (region * rows + lax.div(cells, width)).astype(f32),
            lax.rem(cells, width).astype(f32),
            jnp.where(lane_of((1, slots)) < count, 1.0, 0.0),
        ]
        for i, fact in enumerate(facts):
            board_ref[at + own + i : at + own + i + 1, 0:slots] = fact


def parcel_kernel(site_ref, board_ref, above_ref, below_ref, diffusion_ref, parcel_ref, halo, board):
    own, width = above_ref.shape
    batches, slots = site_ref.shape
    rows = diffusion_ref.shape[0]
    tiles = width // LANES
    for t in range(tiles):
        cols = slice(t * LANES, (t + 1) * LANES)
        halo[t * 24 : t * 24 + own, :] = above_ref[:, cols] * diffusion_ref[0:1, cols]
        halo[(tiles + t) * 24 : (tiles + t) * 24 + own, :] = below_ref[:, cols] * diffusion_ref[rows - 1 : rows, cols]
    halo[2 * tiles * 24 : 2 * tiles * 24 + 24, :] = jnp.zeros((24, LANES), f32)
    lane = lane_of((24, LANES))
    for b in range(batches):
        picked = jnp.zeros((24, LANES), f32)
        for k in range(slots):
            cell = site_ref[b, k]
            col = lax.rem(cell, width)
            row = lax.div(cell, width)
            tile = lax.div(col, LANES)
            block = jnp.where(row == 0, tile, jnp.where(row == rows - 1, tiles + tile, 2 * tiles))
            line = halo[pl.ds(pl.multiple_of(block * 24, 8), 24), :]
            shift = lax.rem(k - lax.rem(col, LANES) + LANES, LANES)
            picked = jnp.where(lane == k, pltpu.roll(line, shift, 1), picked)
        picked = jnp.where(row_of((24, LANES)) < own, picked, 0.0)
        board[b * 32 : b * 32 + 24, :] = board_ref[b * 32 : b * 32 + 24, :] + picked
        board[b * 32 + 24 : b * 32 + 32, :] = board_ref[b * 32 + 24 : b * 32 + 32, :]
    parcel = board[...].T[:slots, :]
    for i in range(parcel_ref.shape[0]):
        parcel_ref[i] = parcel


def finish_kernel(place_ref, partial_ref, above_ref, below_ref, diffusion_ref, stay_ref, near_ref, cross_ref):
    own = above_ref.shape[0]
    rows = diffusion_ref.shape[0]
    tiles = above_ref.shape[1] // LANES // QUARTERS
    size = own * tiles * rows
    row = row_of((rows, LANES))
    for i, (out_ref, base) in enumerate(((stay_ref, 0), (near_ref, 0), (cross_ref, 0), (cross_ref, size))):
        quarter = jnp.bitwise_xor(place_ref[1], i)
        for t in range(tiles):
            cols = pl.ds(pl.multiple_of((quarter * tiles + t) * LANES, LANES), LANES)
            diffusion = diffusion_ref[:, cols]
            first = jnp.where(row == 0, diffusion, 0.0)
            last = jnp.where(row == rows - 1, diffusion, 0.0)
            for e in range(own):
                at = (e * tiles + t) * rows
                part = partial_ref[pl.ds(pl.multiple_of(quarter * size + at, 8), rows), :]
                part = part + first * above_ref[e : e + 1, cols] + last * below_ref[e : e + 1, cols]
                out_ref[base + at : base + at + rows, :] = part


def pack_kernel(place_ref, plane_ref, other_ref, out_ref):
    count, slots, _ = plane_ref.shape
    y = place_ref[3]

    def parcel(o):
        at = y + o
        inside = (at >= 0) & (at < count)
        at = lax.rem(at + count, count)
        return jnp.where(inside, plane_ref[at], other_ref[at])

    lane = lane_of((slots, LANES))
    groups = [parcel(o) for o in (-1, 0, 1)]
    groups.append(jnp.where(lane < 96, parcel(-2), pltpu.roll(parcel(-4), 96, 1)))
    groups.append(jnp.where(lane < 96, parcel(2), pltpu.roll(parcel(4), 96, 1)))
    groups.append(jnp.where(lane < 64, parcel(-3), pltpu.roll(parcel(3), 64, 1)))
    for i in range(out_ref.shape[0]):
        for g, group in enumerate(groups):
            out_ref[i, g * slots : (g + 1) * slots, :] = group


def packed_at(offset, batch):
    if abs(offset) <= 1:
        return offset + 1, batch
    if abs(offset) == 3:
        return 5, batch + (2 if offset > 0 else 0)
    return (3 if offset < 0 else 4), (batch if abs(offset) == 2 else 3)


def beside(hi, lo):
    lane = lane_of(hi.shape)
    again = pltpu.roll(hi, 80, 1)
    last = pltpu.roll(lo, 32, 1)
    first = jnp.where(lane < 80, hi, again)
    second = jnp.where(lane < 32, again, last)
    return jnp.concatenate([first.astype(bf16), second.astype(bf16)], axis=1)


def below_each_other(x):
    hi, lo = halves(x)
    hi, lo = hi.astype(bf16), lo.astype(bf16)
    return jnp.concatenate([hi, lo, hi, jnp.zeros((16, x.shape[1]), bf16)], axis=0)


def update_kernel(
    place_ref, parcels_ref, state0_ref, state1_ref, state2_ref, state3_ref,
    out_ref, obs, inc_ref, ano_ref, gain_lhs, inc_lhs, near_ref, board, state_ref, updated, *, width,
):
    members = 80
    parity = place_ref[0]
    quarter = place_ref[1]
    region = place_ref[2]
    rows, quarter_width = out_ref.shape[1:]
    tiles = quarter_width // LANES
    scale = 1.0 / (RADIUS * RADIUS)
    own = members // QUARTERS
    slots = parcels_ref.shape[1] // 6
    lane = lane_of((slots, LANES))
    blocks = [(o, b) for b in range(4) for o in range(b - 4, 5 - b)]
    for i, (o, b) in enumerate(blocks):
        group, block = packed_at(o, b)
        for p in range(2):
            total = jnp.zeros((slots, LANES), f32)
            for m in range(QUARTERS):
                piece = parcels_ref[p * QUARTERS + m, group * slots : (group + 1) * slots, :]
                moved = pltpu.roll(piece, (own * m - 32 * block) % LANES, 1)
                end = own * (m + 1) + (FACTS if m == QUARTERS - 1 else 0)
                total = jnp.where((lane >= own * m) & (lane < end), moved, total)
            obs[(2 * i + p) * slots : (2 * i + p + 1) * slots, :] = total
    for i, ref in enumerate((state0_ref, state1_ref, state2_ref, state3_ref)):
        size = state0_ref.shape[0]
        at = pl.multiple_of(jnp.bitwise_xor(quarter, i) * size, 8)
        state_ref[pl.ds(at, size), :] = ref[0:size, :]
    starts = [0, 288, 512, 672, 768]
    centres = [96, 64, 32, 0]
    total = starts[-1]
    pick = jnp.where(lane_of((8, LANES)) == members + ROW + row_of((8, LANES)), 1.0, 0.0)
    across = lax.dot_general(
        pick, obs[...], (((1,), (1,)), ((), ())), precision=lax.Precision.HIGHEST, preferred_element_type=f32
    )
    for b in range(4):
        n = starts[b + 1] - starts[b]
        x = obs[starts[b] : starts[b + 1], :]
        member = lane_of((n, LANES)) < members
        fact = lambda i: x[:, members + i : members + i + 1]
        average = jnp.sum(jnp.where(member, x, 0.0), axis=1, keepdims=True) / members
        anomaly = jnp.where(member, x - average, 0.0)
        spread = jnp.sum(anomaly * anomaly, axis=1, keepdims=True) / (members - 1) + epsilon
        live = fact(LIVE)
        noise = jnp.where(live > 0.5, fact(VARIANCE), 1.0)
        posterior = 1.0 / (1.0 / spread + 1.0 / noise)
        post_mean = posterior * (average / spread + fact(READING) / noise)
        increment = post_mean - average + (jnp.sqrt(posterior / spread) - 1.0) * anomaly
        increment = jnp.where(member, increment, 0.0)
        scaled = anomaly * (live / ((members - 1) * spread))
        inc_ref[0:n, :] = increment
        ano_ref[0:n, :] = scaled
        at = centres[b] + 16 * parity
        gain_lhs[b] = beside(*halves(ano_ref[pl.ds(at, 80), :]))
        near_ref[b] = obs[pl.ds(starts[b] + at, 80), :]
        board[...] = jnp.zeros_like(board)
        board[0:80, :] = inc_ref[pl.ds(at, 80), :]
        inc_lhs[b] = beside(*halves(board[...].T[0:80, :]))
        if b < 3:
            y = obs[starts[b + 1] : total, :]
            m = total - starts[b + 1]
            inside = lane_of((m, LANES)) < members
            mean = jnp.sum(jnp.where(inside, y, 0.0), axis=1, keepdims=True) / members
            off = jnp.where(inside, y - mean, 0.0)
            covariance = product(off, scaled, ((1,), (1,)))
            row_gap = y[:, members + ROW : members + ROW + 1] - across[0:1, starts[b] : starts[b + 1]]
            col_gap = jnp.abs(y[:, members + COLUMN : members + COLUMN + 1] - across[1:2, starts[b] : starts[b + 1]])
            col_gap = jnp.minimum(col_gap, width - col_gap)
            remain = jnp.maximum(1.0 - (row_gap * row_gap + col_gap * col_gap) * scale, 0.0)
            weights = remain * remain * covariance
            obs[starts[b + 1] : total, :] = y + product(weights, increment, ((1,), (0,)))
    cols = (lane_of((80, quarter_width)) + quarter * quarter_width).astype(f32)
    closeness = []
    for b in range(4):
        gap = jnp.abs(cols - near_ref[b, :, members + COLUMN : members + COLUMN + 1])
        gap = jnp.minimum(gap, width - gap)
        closeness.append(1.0 - gap * gap * scale)
    together = 4

    def load(first):
        lines = [(r, t) for r in range(first, first + together) for t in range(tiles)]
        return jnp.concatenate([state_ref[pl.ds(t * rows + r, members, stride=tiles * rows), :] for r, t in lines], axis=1)

    def assimilate(state, b, first):
        mean = jnp.mean(state, axis=0, keepdims=True)
        covariance = jnp.dot(gain_lhs[b], below_each_other(state - mean), preferred_element_type=f32)
        tapers = []
        for r in range(first, first + together):
            gap = (region * rows + r).astype(f32) - near_ref[b, :, members + ROW : members + ROW + 1]
            remain = jnp.maximum(closeness[b] - gap * gap * scale, 0.0)
            tapers.append(remain * remain)
        weights = jnp.concatenate(tapers, axis=1) * covariance
        return state + jnp.dot(inc_lhs[b], below_each_other(weights), preferred_element_type=f32)

    for first in range(0, rows, together):
        state = load(first)
        for b in range(4):
            state = assimilate(state, b, first)
        for i in range(together * tiles):
            at = (i % tiles) * rows + first + i // tiles
            updated[pl.ds(at, members, stride=tiles * rows), :] = state[:, i * LANES : (i + 1) * LANES]
    for e in range(members):
        for t in range(tiles):
            at = (e * tiles + t) * rows
            out_ref[e, :, t * LANES : (t + 1) * LANES] = updated[at : at + rows, :]


def local(tracer, diffusion, sites, readings, variances, tally):
    own, rows, width = tracer.shape
    regions = lax.axis_size("region")
    batches, slots = sites.shape
    quarter_width = width // QUARTERS
    members = own * QUARTERS
    region = lax.axis_index("region")
    quarter = lax.axis_index("member")
    vmem = pl.BlockSpec(memory_space=pltpu.VMEM)
    smem = pl.BlockSpec(memory_space=pltpu.SMEM)
    limit = pltpu.CompilerParams(vmem_limit_bytes=32 * 1024 * 1024)
    line = jax.ShapeDtypeStruct((own, width), f32)
    place = jnp.stack([region % 2, quarter, region, region // 2 % RING]).astype(jnp.int32)
    top, bottom = pl.pallas_call(
        edges_kernel, out_shape=(line, line), in_specs=[vmem], out_specs=(vmem, vmem), compiler_params=limit, name="edges"
    )(tracer)
    above = lax.ppermute(bottom, "region", [(i, i + 1) for i in range(regions - 1)])
    below = lax.ppermute(top, "region", [(i + 1, i) for i in range(regions - 1)])
    partial, board = pl.pallas_call(
        step_kernel,
        out_shape=(
            jax.ShapeDtypeStruct((own * rows * width // LANES, LANES), f32),
            jax.ShapeDtypeStruct((LANES, LANES), f32),
        ),
        in_specs=[smem] * 3 + [vmem] * 5,
        out_specs=(vmem, vmem),
        compiler_params=limit,
        cost_estimate=pl.CostEstimate(flops=20_000_000, bytes_accessed=10_000_000, transcendentals=0),
        name="step",
    )(region[None].astype(jnp.int32), sites, tally, tracer, diffusion, sites, readings, variances)
    parcel = pl.pallas_call(
        parcel_kernel,
        out_shape=jax.ShapeDtypeStruct((RING, slots, LANES), f32),
        in_specs=[smem] + [vmem] * 4,
        out_specs=vmem,
        scratch_shapes=[pltpu.VMEM(((2 * width // LANES + 1) * 24, LANES), f32), pltpu.VMEM((LANES, LANES), f32)],
        compiler_params=limit,
        name="parcel",
    )(sites, board, above, below, diffusion)
    planes = regions // 2 // RING
    rings = [[(z * RING + y) * 2 + p for y in range(RING)] for z in range(planes) for p in range(2)]
    plane = lax.all_to_all(parcel, "region", 0, 0, axis_index_groups=rings)
    size = own * rows * quarter_width // LANES
    stay, near, cross = pl.pallas_call(
        finish_kernel,
        out_shape=[jax.ShapeDtypeStruct((n * size, LANES), f32) for n in (1, 1, 2)],
        in_specs=[smem] + [vmem] * 4,
        out_specs=[vmem] * 3,
        compiler_params=limit,
        cost_estimate=pl.CostEstimate(flops=2_000_000, bytes_accessed=4_000_000, transcendentals=0),
        name="finish",
    )(place, partial, above, below, diffusion)
    crossed = lax.ppermute(cross, "member", [(m, m ^ 2) for m in range(QUARTERS)])
    plane, _ = lax.optimization_barrier((plane, stay))
    to_core = [(m, m ^ 1) for m in range(QUARTERS)]
    states = [stay, lax.ppermute(near, "member", to_core), crossed, lax.ppermute(crossed[size:], "member", to_core)]
    swap = []
    for z in range(planes):
        for y in range(RING):
            to = z + (1 if y >= RING // 2 else -1)
            if 0 <= to < planes:
                swap += [((z * RING + y) * 2 + p, (to * RING + RING - 1 - y) * 2 + p) for p in range(2)]
    other = lax.ppermute(plane, "region", swap)
    packed = pl.pallas_call(
        pack_kernel,
        out_shape=jax.ShapeDtypeStruct((2 * QUARTERS, 6 * slots, LANES), f32),
        in_specs=[smem] + [vmem] * 2,
        out_specs=vmem,
        compiler_params=limit,
        name="pack",
    )(place, plane, other)
    packed, _ = lax.optimization_barrier((packed, crossed))
    lines = [[2 * QUARTERS * g + i for i in range(2 * QUARTERS)] for g in range(regions // 2)]
    parcels = lax.all_to_all(packed, ("region", "member"), 0, 0, axis_index_groups=lines)
    block = 2 * slots
    total = 24 * block
    return pl.pallas_call(
        functools.partial(update_kernel, width=width),
        out_shape=jax.ShapeDtypeStruct((members, rows, quarter_width), f32),
        in_specs=[smem] + [vmem] * 5,
        out_specs=vmem,
        scratch_shapes=[
            pltpu.VMEM((total, LANES), f32),
            pltpu.VMEM((9 * block, LANES), f32),
            pltpu.VMEM((9 * block, LANES), f32),
            pltpu.VMEM((4, 80, 256), bf16),
            pltpu.VMEM((4, 80, 256), bf16),
            pltpu.VMEM((4, 80, LANES), f32),
            pltpu.VMEM((LANES, LANES), f32),
            pltpu.VMEM((members * rows * quarter_width // LANES, LANES), f32),
            pltpu.VMEM((members * rows * quarter_width // LANES, LANES), f32),
        ],
        compiler_params=limit,
        name="update",
    )(place, parcels, *states)


def solution(mesh):
    placed = (
        P("member", "region", None),
        P("region", None),
        P(None, "region"),
        P(None, "region"),
        P(None, "region"),
        P(),
    )
    return jax.shard_map(
        local, mesh=mesh, in_specs=placed, out_specs=P(None, "region", "member"), check_vma=False
    )
```

```python
import functools

import jax
import jax.numpy as jnp
from jax import lax
from jax.experimental import pallas as pl
from jax.experimental.pallas import tpu as pltpu
from jax.sharding import PartitionSpec as P

REACH = 2
RADIUS = 16
epsilon = 1e-05
LANES = 128
QUARTERS = 4
RING = 8
f32 = jnp.float32
bf16 = jnp.bfloat16

FACTS = 5
READING, VARIANCE, ROW, COLUMN, LIVE = range(FACTS)


def lane_of(shape):
    return lax.broadcasted_iota(jnp.int32, shape, len(shape) - 1)


def row_of(shape):
    return lax.broadcasted_iota(jnp.int32, shape, len(shape) - 2)


def halves(x):
    hi = x.astype(bf16).astype(f32)
    return hi, x - hi


def product(a, b, dims):
    a_hi, a_lo = [v.astype(bf16) for v in halves(a)]
    b_hi, b_lo = [v.astype(bf16) for v in halves(b)]
    dot = functools.partial(lax.dot_general, dimension_numbers=(dims, ((), ())), preferred_element_type=f32)
    return dot(a_hi, b_hi) + (dot(a_hi, b_lo) + dot(a_lo, b_hi))


def edges_kernel(tracer_ref, top_ref, bottom_ref):
    own, rows, _ = tracer_ref.shape
    for e in range(own):
        top_ref[e : e + 1, :] = tracer_ref[e, 0:1, :]
        bottom_ref[e : e + 1, :] = tracer_ref[e, rows - 1 : rows, :]


def step_kernel(
    region_ref, site_ref, tally_ref, tracer_ref, diffusion_ref, site_vec_ref, reading_ref, variance_ref,
    partial_ref, board_ref,
):
    own, rows, width = tracer_ref.shape
    batches, slots = site_ref.shape
    tiles = width // LANES // QUARTERS
    region = region_ref[0]
    diffusion = diffusion_ref[...]
    row = row_of((rows, width))
    for e in range(own):
        x = tracer_ref[e]
        lower = jnp.where(row == 0, 0.0, pltpu.roll(x, 1, 0))
        upper = jnp.where(row == rows - 1, 0.0, pltpu.roll(x, rows - 1, 0))
        east = pltpu.roll(x, width - 1, 1)
        west = pltpu.roll(x, 1, 1)
        y = x + diffusion * (upper + lower + east + west - 4.0 * x)
        for q in range(QUARTERS):
            for t in range(tiles):
                at = ((q * own + e) * tiles + t) * rows
                col = (q * tiles + t) * LANES
                partial_ref[at : at + rows, :] = y[:, col : col + LANES]
    board_ref[...] = jnp.zeros_like(board_ref)
    lane = lane_of((own, LANES))
    for b in range(batches):
        picked = jnp.zeros((own, LANES), f32)
        for k in range(slots):
            cell = site_ref[b, k]
            col = lax.rem(cell, width)
            tile = lax.div(col, LANES)
            start = lax.div(tile, tiles) * (own * tiles * rows) + lax.rem(tile, tiles) * rows + lax.div(cell, width)
            line = partial_ref[pl.ds(start, own, stride=tiles * rows), :]
            shift = lax.rem(k - lax.rem(col, LANES) + LANES, LANES)
            picked = jnp.where(lane == k, pltpu.roll(line, shift, 1), picked)
        at = b * 32
        board_ref[at : at + own, :] = picked
        cells = site_vec_ref[b : b + 1, :]
        count = tally_ref[b, region]
        facts = [
            reading_ref[b : b + 1, :],
            variance_ref[b : b + 1, :],
            (region * rows + lax.div(cells, width)).astype(f32),
            lax.rem(cells, width).astype(f32),
            jnp.where(lane_of((1, slots)) < count, 1.0, 0.0),
        ]
        for i, fact in enumerate(facts):
            board_ref[at + own + i : at + own + i + 1, 0:slots] = fact


def parcel_kernel(site_ref, board_ref, above_ref, below_ref, diffusion_ref, parcel_ref, halo, board):
    own, width = above_ref.shape
    batches, slots = site_ref.shape
    rows = diffusion_ref.shape[0]
    tiles = width // LANES
    for t in range(tiles):
        cols = slice(t * LANES, (t + 1) * LANES)
        halo[t * 24 : t * 24 + own, :] = above_ref[:, cols] * diffusion_ref[0:1, cols]
        halo[(tiles + t) * 24 : (tiles + t) * 24 + own, :] = below_ref[:, cols] * diffusion_ref[rows - 1 : rows, cols]
    halo[2 * tiles * 24 : 2 * tiles * 24 + 24, :] = jnp.zeros((24, LANES), f32)
    lane = lane_of((24, LANES))
    for b in range(batches):
        picked = jnp.zeros((24, LANES), f32)
        for k in range(slots):
            cell = site_ref[b, k]
            col = lax.rem(cell, width)
            row = lax.div(cell, width)
            tile = lax.div(col, LANES)
            block = jnp.where(row == 0, tile, jnp.where(row == rows - 1, tiles + tile, 2 * tiles))
            line = halo[pl.ds(pl.multiple_of(block * 24, 8), 24), :]
            shift = lax.rem(k - lax.rem(col, LANES) + LANES, LANES)
            picked = jnp.where(lane == k, pltpu.roll(line, shift, 1), picked)
        picked = jnp.where(row_of((24, LANES)) < own, picked, 0.0)
        board[b * 32 : b * 32 + 24, :] = board_ref[b * 32 : b * 32 + 24, :] + picked
        board[b * 32 + 24 : b * 32 + 32, :] = board_ref[b * 32 + 24 : b * 32 + 32, :]
    parcel_ref[...] = board[...].T[:slots, :]


def repeat_kernel(own_ref, other_ref, out_ref):
    slots = own_ref.shape[0]
    for i in range(out_ref.shape[0]):
        out_ref[i, 0:slots, :] = own_ref[...]
        out_ref[i, slots : 2 * slots, :] = other_ref[...]


def finish_kernel(place_ref, partial_ref, above_ref, below_ref, diffusion_ref, stay_ref, near_ref, cross_ref):
    own = above_ref.shape[0]
    rows = diffusion_ref.shape[0]
    tiles = above_ref.shape[1] // LANES // QUARTERS
    size = own * tiles * rows
    row = row_of((rows, LANES))
    for i, (out_ref, base) in enumerate(((stay_ref, 0), (near_ref, 0), (cross_ref, 0), (cross_ref, size))):
        quarter = jnp.bitwise_xor(place_ref[1], i)
        for t in range(tiles):
            cols = pl.ds(pl.multiple_of((quarter * tiles + t) * LANES, LANES), LANES)
            diffusion = diffusion_ref[:, cols]
            first = jnp.where(row == 0, diffusion, 0.0)
            last = jnp.where(row == rows - 1, diffusion, 0.0)
            for e in range(own):
                at = (e * tiles + t) * rows
                part = partial_ref[pl.ds(pl.multiple_of(quarter * size + at, 8), rows), :]
                part = part + first * above_ref[e : e + 1, cols] + last * below_ref[e : e + 1, cols]
                out_ref[base + at : base + at + rows, :] = part


def pack_kernel(place_ref, plane_ref, out_ref):
    count = plane_ref.shape[0]
    slots = plane_ref.shape[1] // 2
    y = place_ref[3]

    def parcel(o):
        at = y + o
        inside = (at >= 0) & (at < count)
        at = lax.rem(at + count, count)
        return jnp.where(inside, plane_ref[at, 0:slots], plane_ref[count - 1 - at, slots : 2 * slots])

    lane = lane_of((slots, LANES))
    groups = [parcel(o) for o in (-1, 0, 1)]
    groups.append(jnp.where(lane < 96, parcel(-2), pltpu.roll(parcel(-4), 96, 1)))
    groups.append(jnp.where(lane < 96, parcel(2), pltpu.roll(parcel(4), 96, 1)))
    groups.append(jnp.where(lane < 64, parcel(-3), pltpu.roll(parcel(3), 64, 1)))
    for i in range(out_ref.shape[0]):
        for g, group in enumerate(groups):
            out_ref[i, g * slots : (g + 1) * slots, :] = group


def packed_at(offset, batch):
    if abs(offset) <= 1:
        return offset + 1, batch
    if abs(offset) == 3:
        return 5, batch + (2 if offset > 0 else 0)
    return (3 if offset < 0 else 4), (batch if abs(offset) == 2 else 3)


def beside(hi, lo):
    lane = lane_of(hi.shape)
    again = pltpu.roll(hi, 80, 1)
    last = pltpu.roll(lo, 32, 1)
    first = jnp.where(lane < 80, hi, again)
    second = jnp.where(lane < 32, again, last)
    return jnp.concatenate([first.astype(bf16), second.astype(bf16)], axis=1)


def below_each_other(x):
    hi, lo = halves(x)
    hi, lo = hi.astype(bf16), lo.astype(bf16)
    return jnp.concatenate([hi, lo, hi, jnp.zeros((16, x.shape[1]), bf16)], axis=0)


def update_kernel(
    place_ref, parcels_ref, state0_ref, state1_ref, state2_ref, state3_ref,
    out_ref, obs, inc_ref, ano_ref, gain_lhs, inc_lhs, near_ref, board, state_ref, updated, whole, centre_ref, sems, *, width,
):
    members = 80
    parity = place_ref[0]
    quarter = place_ref[1]
    region = place_ref[2]
    rows, quarter_width = out_ref.shape[1:]
    tiles = quarter_width // LANES
    scale = 1.0 / (RADIUS * RADIUS)
    own = members // QUARTERS
    slots = parcels_ref.shape[1] // 6
    lane = lane_of((slots, LANES))
    blocks = [(o, b) for b in range(4) for o in range(b - 4, 5 - b)]
    for i, (o, b) in enumerate(blocks):
        group, block = packed_at(o, b)
        for p in range(2):
            total = jnp.zeros((slots, LANES), f32)
            for m in range(QUARTERS):
                piece = parcels_ref[p * QUARTERS + m, group * slots : (group + 1) * slots, :]
                moved = pltpu.roll(piece, (own * m - 32 * block) % LANES, 1)
                end = own * (m + 1) + (FACTS if m == QUARTERS - 1 else 0)
                total = jnp.where((lane >= own * m) & (lane < end), moved, total)
            obs[(2 * i + p) * slots : (2 * i + p + 1) * slots, :] = total
    for i, ref in enumerate((state0_ref, state1_ref, state2_ref, state3_ref)):
        size = state0_ref.shape[0]
        at = pl.multiple_of(jnp.bitwise_xor(quarter, i) * size, 8)
        state_ref[pl.ds(at, size), :] = ref[0:size, :]
    starts = [0, 288, 512, 672, 768]
    centres = [96, 64, 32, 0]
    total = starts[-1]
    pick = jnp.where(lane_of((8, LANES)) == members + ROW + row_of((8, LANES)), 1.0, 0.0).astype(bf16)
    across = sum(
        lax.dot_general(pick, half.astype(bf16), (((1,), (1,)), ((), ())), preferred_element_type=f32)
        for half in halves(obs[...])
    )
    everything = obs[...]
    inside = lane_of(everything.shape) < members
    centre = jnp.sum(jnp.where(inside, everything, 0.0), axis=1, keepdims=True) / members
    centre_ref[...] = jnp.broadcast_to(centre, everything.shape)
    obs[...] = jnp.where(inside, everything - centre, everything)
    for b in range(4):
        n = starts[b + 1] - starts[b]
        x = obs[starts[b] : starts[b + 1], :]
        member = lane_of((n, LANES)) < members
        fact = lambda i: x[:, members + i : members + i + 1]
        shift = jnp.sum(jnp.where(member, x, 0.0), axis=1, keepdims=True) / members
        anomaly = jnp.where(member, x - shift, 0.0)
        average = centre_ref[starts[b] : starts[b + 1], 0:1] + shift
        spread = jnp.sum(anomaly * anomaly, axis=1, keepdims=True) / (members - 1) + epsilon
        live = fact(LIVE)
        noise = jnp.where(live > 0.5, fact(VARIANCE), 1.0)
        share = 1.0 / (spread + noise)
        increment = spread * share * (fact(READING) - average) + (jnp.sqrt(noise * share) - 1.0) * anomaly
        increment = jnp.where(member, increment, 0.0)
        scaled = anomaly * (live / ((members - 1) * spread))
        inc_ref[0:n, :] = increment
        ano_ref[0:n, :] = scaled
        at = centres[b] + 16 * parity
        gain_lhs[b] = beside(*halves(ano_ref[pl.ds(at, 80), :]))
        near_ref[b] = obs[pl.ds(starts[b] + at, 80), :]
        board[...] = jnp.zeros_like(board)
        board[0:80, :] = inc_ref[pl.ds(at, 80), :]
        inc_lhs[b] = beside(*halves(board[...].T[0:80, :]))
        if b < 3:
            y = obs[starts[b + 1] : total, :]
            m = total - starts[b + 1]
            covariance = product(jnp.where(lane_of((m, LANES)) < members, y, 0.0), scaled, ((1,), (1,)))
            row_gap = y[:, members + ROW : members + ROW + 1] - across[0:1, starts[b] : starts[b + 1]]
            col_gap = jnp.abs(y[:, members + COLUMN : members + COLUMN + 1] - across[1:2, starts[b] : starts[b + 1]])
            col_gap = jnp.minimum(col_gap, width - col_gap)
            remain = jnp.maximum(1.0 - (row_gap * row_gap + col_gap * col_gap) * scale, 0.0)
            weights = remain * remain * covariance
            obs[starts[b + 1] : total, :] = y + product(weights, increment, ((1,), (0,)))
    cols = (lane_of((80, quarter_width)) + quarter * quarter_width).astype(f32)
    closeness = []
    for b in range(4):
        gap = jnp.abs(cols - near_ref[b, :, members + COLUMN : members + COLUMN + 1])
        gap = jnp.minimum(gap, width - gap)
        closeness.append(1.0 - gap * gap * scale)
    together = 2

    def load(first):
        lines = [(r, t) for t in range(first, first + together) for r in range(rows)]
        return jnp.concatenate([state_ref[pl.ds(t * rows + r, members, stride=tiles * rows), :] for r, t in lines], axis=1)

    def assimilate(state, b, first):
        covariance = jnp.dot(gain_lhs[b], below_each_other(state), preferred_element_type=f32)
        tapers = []
        for t in range(first, first + together):
            near = closeness[b][:, t * LANES : (t + 1) * LANES]
            for r in range(rows):
                gap = (region * rows + r).astype(f32) - near_ref[b, :, members + ROW : members + ROW + 1]
                remain = jnp.maximum(near - gap * gap * scale, 0.0)
                tapers.append(remain * remain)
        weights = jnp.concatenate(tapers, axis=1) * covariance
        return state + jnp.dot(inc_lhs[b], below_each_other(weights), preferred_element_type=f32)

    copies = []
    for first in range(0, tiles, together):
        state = load(first)
        centre = jnp.mean(state, axis=0, keepdims=True)
        state = state - centre
        for b in range(4):
            state = assimilate(state, b, first)
        state = state + centre
        for i in range(together * rows):
            t, r = first + i // rows, i % rows
            updated[(t * rows + r) * members : (t * rows + r + 1) * members, :] = state[:, i * LANES : (i + 1) * LANES]
        cols = slice(first * LANES, (first + together) * LANES)
        for e in range(members):
            for t in range(first, first + together):
                line = updated[pl.ds(t * rows * members + e, rows, stride=members), :]
                whole[e, :, t * LANES : (t + 1) * LANES] = line
        copies.append(pltpu.make_async_copy(whole.at[:, :, cols], out_ref.at[:, :, cols], sems.at[first // together]))
        copies[-1].start()
    for copy in copies:
        copy.wait()


def local(tracer, diffusion, sites, readings, variances, tally):
    own, rows, width = tracer.shape
    regions = lax.axis_size("region")
    batches, slots = sites.shape
    quarter_width = width // QUARTERS
    members = own * QUARTERS
    region = lax.axis_index("region")
    quarter = lax.axis_index("member")
    vmem = pl.BlockSpec(memory_space=pltpu.VMEM)
    smem = pl.BlockSpec(memory_space=pltpu.SMEM)
    limit = pltpu.CompilerParams(vmem_limit_bytes=32 * 1024 * 1024)
    line = jax.ShapeDtypeStruct((own, width), f32)
    place = jnp.stack([region % 2, quarter, region, region // 2 % RING]).astype(jnp.int32)
    top, bottom = pl.pallas_call(
        edges_kernel, out_shape=(line, line), in_specs=[vmem], out_specs=(vmem, vmem), compiler_params=limit, name="edges"
    )(tracer)
    above = lax.ppermute(bottom, "region", [(i, i + 1) for i in range(regions - 1)])
    below = lax.ppermute(top, "region", [(i + 1, i) for i in range(regions - 1)])
    partial, board = pl.pallas_call(
        step_kernel,
        out_shape=(
            jax.ShapeDtypeStruct((own * rows * width // LANES, LANES), f32),
            jax.ShapeDtypeStruct((LANES, LANES), f32),
        ),
        in_specs=[smem] * 3 + [vmem] * 5,
        out_specs=(vmem, vmem),
        compiler_params=limit,
        cost_estimate=pl.CostEstimate(flops=20_000_000, bytes_accessed=10_000_000, transcendentals=0),
        name="step",
    )(region[None].astype(jnp.int32), sites, tally, tracer, diffusion, sites, readings, variances)
    parcel = pl.pallas_call(
        parcel_kernel,
        out_shape=jax.ShapeDtypeStruct((slots, LANES), f32),
        in_specs=[smem] + [vmem] * 4,
        out_specs=vmem,
        scratch_shapes=[pltpu.VMEM(((2 * width // LANES + 1) * 24, LANES), f32), pltpu.VMEM((LANES, LANES), f32)],
        compiler_params=limit,
        name="parcel",
    )(sites, board, above, below, diffusion)
    parcel, partial = lax.optimization_barrier((parcel, partial))
    planes = regions // 2 // RING
    swap = []
    for z in range(planes):
        for y in range(RING):
            to = z + (1 if y >= RING // 2 else -1)
            if 0 <= to < planes:
                swap += [((z * RING + y) * 2 + p, (to * RING + RING - 1 - y) * 2 + p) for p in range(2)]
    other = lax.ppermute(parcel, "region", swap)
    size = own * rows * quarter_width // LANES
    stay, near, cross = pl.pallas_call(
        finish_kernel,
        out_shape=[jax.ShapeDtypeStruct((n * size, LANES), f32) for n in (1, 1, 2)],
        in_specs=[smem] + [vmem] * 4,
        out_specs=[vmem] * 3,
        compiler_params=limit,
        cost_estimate=pl.CostEstimate(flops=10_000_000_000, bytes_accessed=4_000_000, transcendentals=0),
        name="finish",
    )(place, partial, above, below, diffusion)
    crossed = lax.ppermute(cross, "member", [(m, m ^ 2) for m in range(QUARTERS)])
    other, _ = lax.optimization_barrier((other, stay))
    repeated = pl.pallas_call(
        repeat_kernel,
        out_shape=jax.ShapeDtypeStruct((RING, 2 * slots, LANES), f32),
        in_specs=[vmem] * 2,
        out_specs=vmem,
        compiler_params=limit,
        cost_estimate=pl.CostEstimate(flops=50_000_000_000, bytes_accessed=2_000_000, transcendentals=0),
        name="repeat",
    )(parcel, other)
    rings = [[(z * RING + y) * 2 + p for y in range(RING)] for z in range(planes) for p in range(2)]
    plane = lax.all_to_all(repeated, "region", 0, 0, axis_index_groups=rings)
    to_core = [(m, m ^ 1) for m in range(QUARTERS)]
    states = [stay, lax.ppermute(near, "member", to_core), crossed, lax.ppermute(crossed[size:], "member", to_core)]
    packed = pl.pallas_call(
        pack_kernel,
        out_shape=jax.ShapeDtypeStruct((2 * QUARTERS, 6 * slots, LANES), f32),
        in_specs=[smem, vmem],
        out_specs=vmem,
        compiler_params=limit,
        cost_estimate=pl.CostEstimate(flops=1_000_000, bytes_accessed=2_000_000, transcendentals=0),
        name="pack",
    )(place, plane)
    lines = [[2 * QUARTERS * g + i for i in range(2 * QUARTERS)] for g in range(regions // 2)]
    parcels = lax.all_to_all(packed, ("region", "member"), 0, 0, axis_index_groups=lines)
    block = 2 * slots
    total = 24 * block
    return pl.pallas_call(
        functools.partial(update_kernel, width=width),
        out_shape=jax.ShapeDtypeStruct((members, rows, quarter_width), f32),
        in_specs=[smem] + [vmem] * 5,
        out_specs=pl.BlockSpec(memory_space=pl.ANY),
        scratch_shapes=[
            pltpu.VMEM((total, LANES), f32),
            pltpu.VMEM((9 * block, LANES), f32),
            pltpu.VMEM((9 * block, LANES), f32),
            pltpu.VMEM((4, 80, 256), bf16),
            pltpu.VMEM((4, 80, 256), bf16),
            pltpu.VMEM((4, 80, LANES), f32),
            pltpu.VMEM((LANES, LANES), f32),
            pltpu.VMEM((members * rows * quarter_width // LANES, LANES), f32),
            pltpu.VMEM((members * rows * quarter_width // LANES, LANES), f32),
            pltpu.VMEM((members, rows, quarter_width), f32),
            pltpu.VMEM((total, LANES), f32),
            pltpu.SemaphoreType.DMA((2,)),
        ],
        compiler_params=limit,
        name="update",
    )(place, parcels, *states)


def solution(mesh):
    placed = (
        P("member", "region", None),
        P("region", None),
        P(None, "region"),
        P(None, "region"),
        P(None, "region"),
        P(),
    )
    return jax.shard_map(
        local, mesh=mesh, in_specs=placed, out_specs=P(None, "region", "member"), check_vma=False
    )
```

```python
import functools

import jax
import jax.numpy as jnp
from jax import lax
from jax.experimental import pallas as pl
from jax.experimental.pallas import tpu as pltpu
from jax.sharding import PartitionSpec as P

REACH = 2
RADIUS = 16
epsilon = 1e-05
LANES = 128
QUARTERS = 4
RING = 8
f32 = jnp.float32
bf16 = jnp.bfloat16

FACTS = 5
READING, VARIANCE, ROW, COLUMN, LIVE = range(FACTS)


def lane_of(shape):
    return lax.broadcasted_iota(jnp.int32, shape, len(shape) - 1)


def row_of(shape):
    return lax.broadcasted_iota(jnp.int32, shape, len(shape) - 2)


def halves(x):
    hi = x.astype(bf16).astype(f32)
    return hi, x - hi


def product(a, b, dims):
    a_hi, a_lo = [v.astype(bf16) for v in halves(a)]
    b_hi, b_lo = [v.astype(bf16) for v in halves(b)]
    dot = functools.partial(lax.dot_general, dimension_numbers=(dims, ((), ())), preferred_element_type=f32)
    return dot(a_hi, b_hi) + (dot(a_hi, b_lo) + dot(a_lo, b_hi))


def edges_kernel(tracer_ref, top_ref, bottom_ref):
    own, rows, _ = tracer_ref.shape
    for e in range(own):
        top_ref[e : e + 1, :] = tracer_ref[e, 0:1, :]
        bottom_ref[e : e + 1, :] = tracer_ref[e, rows - 1 : rows, :]


def step_kernel(
    region_ref, site_ref, tally_ref, tracer_ref, diffusion_ref, site_vec_ref, reading_ref, variance_ref,
    partial_ref, board_ref,
):
    own, rows, width = tracer_ref.shape
    batches, slots = site_ref.shape
    tiles = width // LANES // QUARTERS
    region = region_ref[0]
    diffusion = diffusion_ref[...]
    row = row_of((rows, width))
    for e in range(own):
        x = tracer_ref[e]
        lower = jnp.where(row == 0, 0.0, pltpu.roll(x, 1, 0))
        upper = jnp.where(row == rows - 1, 0.0, pltpu.roll(x, rows - 1, 0))
        east = pltpu.roll(x, width - 1, 1)
        west = pltpu.roll(x, 1, 1)
        y = x + diffusion * (upper + lower + east + west - 4.0 * x)
        for q in range(QUARTERS):
            for t in range(tiles):
                at = ((q * own + e) * tiles + t) * rows
                col = (q * tiles + t) * LANES
                partial_ref[at : at + rows, :] = y[:, col : col + LANES]
    board_ref[...] = jnp.zeros_like(board_ref)
    lane = lane_of((own, LANES))
    for b in range(batches):
        picked = jnp.zeros((own, LANES), f32)
        for k in range(slots):
            cell = site_ref[b, k]
            col = lax.rem(cell, width)
            tile = lax.div(col, LANES)
            start = lax.div(tile, tiles) * (own * tiles * rows) + lax.rem(tile, tiles) * rows + lax.div(cell, width)
            line = partial_ref[pl.ds(start, own, stride=tiles * rows), :]
            shift = lax.rem(k - lax.rem(col, LANES) + LANES, LANES)
            picked = jnp.where(lane == k, pltpu.roll(line, shift, 1), picked)
        at = b * 32
        board_ref[at : at + own, :] = picked
        cells = site_vec_ref[b : b + 1, :]
        count = tally_ref[b, region]
        facts = [
            reading_ref[b : b + 1, :],
            variance_ref[b : b + 1, :],
            (region * rows + lax.div(cells, width)).astype(f32),
            lax.rem(cells, width).astype(f32),
            jnp.where(lane_of((1, slots)) < count, 1.0, 0.0),
        ]
        for i, fact in enumerate(facts):
            board_ref[at + own + i : at + own + i + 1, 0:slots] = fact


def parcel_kernel(site_ref, board_ref, above_ref, below_ref, diffusion_ref, parcel_ref, halo, board):
    own, width = above_ref.shape
    batches, slots = site_ref.shape
    rows = diffusion_ref.shape[0]
    tiles = width // LANES
    for t in range(tiles):
        cols = slice(t * LANES, (t + 1) * LANES)
        halo[t * 24 : t * 24 + own, :] = above_ref[:, cols] * diffusion_ref[0:1, cols]
        halo[(tiles + t) * 24 : (tiles + t) * 24 + own, :] = below_ref[:, cols] * diffusion_ref[rows - 1 : rows, cols]
    halo[2 * tiles * 24 : 2 * tiles * 24 + 24, :] = jnp.zeros((24, LANES), f32)
    lane = lane_of((24, LANES))
    for b in range(batches):
        picked = jnp.zeros((24, LANES), f32)
        for k in range(slots):
            cell = site_ref[b, k]
            col = lax.rem(cell, width)
            row = lax.div(cell, width)
            tile = lax.div(col, LANES)
            block = jnp.where(row == 0, tile, jnp.where(row == rows - 1, tiles + tile, 2 * tiles))
            line = halo[pl.ds(pl.multiple_of(block * 24, 8), 24), :]
            shift = lax.rem(k - lax.rem(col, LANES) + LANES, LANES)
            picked = jnp.where(lane == k, pltpu.roll(line, shift, 1), picked)
        picked = jnp.where(row_of((24, LANES)) < own, picked, 0.0)
        board[b * 32 : b * 32 + 24, :] = board_ref[b * 32 : b * 32 + 24, :] + picked
        board[b * 32 + 24 : b * 32 + 32, :] = board_ref[b * 32 + 24 : b * 32 + 32, :]
    parcel_ref[...] = board[...].T[:slots, :]


def repeat_kernel(own_ref, other_ref, out_ref):
    slots = own_ref.shape[0]
    for i in range(out_ref.shape[0]):
        out_ref[i, 0:slots, :] = own_ref[...]
        out_ref[i, slots : 2 * slots, :] = other_ref[...]


def finish_kernel(place_ref, partial_ref, above_ref, below_ref, diffusion_ref, stay_ref, near_ref, cross_ref):
    own = above_ref.shape[0]
    rows = diffusion_ref.shape[0]
    tiles = above_ref.shape[1] // LANES // QUARTERS
    size = own * tiles * rows
    row = row_of((rows, LANES))
    for i, (out_ref, base) in enumerate(((stay_ref, 0), (near_ref, 0), (cross_ref, 0), (cross_ref, size))):
        quarter = jnp.bitwise_xor(place_ref[1], i)
        for t in range(tiles):
            cols = pl.ds(pl.multiple_of((quarter * tiles + t) * LANES, LANES), LANES)
            diffusion = diffusion_ref[:, cols]
            first = jnp.where(row == 0, diffusion, 0.0)
            last = jnp.where(row == rows - 1, diffusion, 0.0)
            for e in range(own):
                at = (e * tiles + t) * rows
                part = partial_ref[pl.ds(pl.multiple_of(quarter * size + at, 8), rows), :]
                part = part + first * above_ref[e : e + 1, cols] + last * below_ref[e : e + 1, cols]
                out_ref[base + at : base + at + rows, :] = part


def pack_kernel(place_ref, plane_ref, out_ref):
    count = plane_ref.shape[0]
    slots = plane_ref.shape[1] // 2
    y = place_ref[3]

    def parcel(o):
        at = y + o
        inside = (at >= 0) & (at < count)
        at = lax.rem(at + count, count)
        return jnp.where(inside, plane_ref[at, 0:slots], plane_ref[count - 1 - at, slots : 2 * slots])

    lane = lane_of((slots, LANES))
    groups = [parcel(o) for o in (-1, 0, 1)]
    groups.append(jnp.where(lane < 96, parcel(-2), pltpu.roll(parcel(-4), 96, 1)))
    groups.append(jnp.where(lane < 96, parcel(2), pltpu.roll(parcel(4), 96, 1)))
    groups.append(jnp.where(lane < 64, parcel(-3), pltpu.roll(parcel(3), 64, 1)))
    for i in range(out_ref.shape[0]):
        for g, group in enumerate(groups):
            out_ref[i, g * slots : (g + 1) * slots, :] = group


def packed_at(offset, batch):
    if abs(offset) <= 1:
        return offset + 1, batch
    if abs(offset) == 3:
        return 5, batch + (2 if offset > 0 else 0)
    return (3 if offset < 0 else 4), (batch if abs(offset) == 2 else 3)


def beside(hi, lo):
    lane = lane_of(hi.shape)
    again = pltpu.roll(hi, 80, 1)
    last = pltpu.roll(lo, 32, 1)
    first = jnp.where(lane < 80, hi, again)
    second = jnp.where(lane < 32, again, last)
    return jnp.concatenate([first.astype(bf16), second.astype(bf16)], axis=1)


def below_each_other(x):
    hi, lo = halves(x)
    hi, lo = hi.astype(bf16), lo.astype(bf16)
    return jnp.concatenate([hi, lo, hi, jnp.zeros((16, x.shape[1]), bf16)], axis=0)


def update_kernel(
    place_ref, parcels_ref, state0_ref, state1_ref, state2_ref, state3_ref,
    out_ref, obs, inc_ref, ano_ref, gain_lhs, inc_lhs, near_ref, board, state_ref, updated, whole, centre_ref, sems, *, width,
):
    members = 80
    parity = place_ref[0]
    quarter = place_ref[1]
    region = place_ref[2]
    rows, quarter_width = out_ref.shape[1:]
    tiles = quarter_width // LANES
    scale = 1.0 / (RADIUS * RADIUS)
    own = members // QUARTERS
    slots = parcels_ref.shape[1] // 6
    lane = lane_of((slots, LANES))
    blocks = [(o, b) for b in range(4) for o in range(b - 4, 5 - b)]
    for i, (o, b) in enumerate(blocks):
        group, block = packed_at(o, b)
        for p in range(2):
            total = jnp.zeros((slots, LANES), f32)
            for m in range(QUARTERS):
                piece = parcels_ref[p * QUARTERS + m, group * slots : (group + 1) * slots, :]
                moved = pltpu.roll(piece, (own * m - 32 * block) % LANES, 1)
                end = own * (m + 1) + (FACTS if m == QUARTERS - 1 else 0)
                total = jnp.where((lane >= own * m) & (lane < end), moved, total)
            obs[(2 * i + p) * slots : (2 * i + p + 1) * slots, :] = total
    for i, ref in enumerate((state0_ref, state1_ref, state2_ref, state3_ref)):
        size = state0_ref.shape[0]
        at = pl.multiple_of(jnp.bitwise_xor(quarter, i) * size, 8)
        state_ref[pl.ds(at, size), :] = ref[0:size, :]
    starts = [0, 288, 512, 672, 768]
    centres = [96, 64, 32, 0]
    total = starts[-1]
    pick = jnp.where(lane_of((8, LANES)) == members + ROW + row_of((8, LANES)), 1.0, 0.0).astype(bf16)
    across = sum(
        lax.dot_general(pick, half.astype(bf16), (((1,), (1,)), ((), ())), preferred_element_type=f32)
        for half in halves(obs[...])
    )
    everything = obs[...]
    inside = lane_of(everything.shape) < members
    centre = jnp.sum(jnp.where(inside, everything, 0.0), axis=1, keepdims=True) / members
    centre_ref[...] = jnp.broadcast_to(centre, everything.shape)
    obs[...] = jnp.where(inside, everything - centre, everything)
    cols = (lane_of((80, quarter_width)) + quarter * quarter_width).astype(f32)
    closeness = {}
    together = 4

    def load(first):
        lines = [(r, t) for t in range(first, first + together) for r in range(rows)]
        return jnp.concatenate([state_ref[pl.ds(t * rows + r, members, stride=tiles * rows), :] for r, t in lines], axis=1)

    def assimilate(state, b, first):
        covariance = jnp.dot(gain_lhs[b], below_each_other(state), preferred_element_type=f32)
        tapers = []
        for t in range(first, first + together):
            near = closeness[b][:, t * LANES : (t + 1) * LANES]
            for r in range(rows):
                gap = (region * rows + r).astype(f32) - near_ref[b, :, members + ROW : members + ROW + 1]
                remain = jnp.maximum(near - gap * gap * scale, 0.0)
                tapers.append(remain * remain)
        weights = jnp.concatenate(tapers, axis=1) * covariance
        return state + jnp.dot(inc_lhs[b], below_each_other(weights), preferred_element_type=f32)

    firsts = range(0, tiles, together)
    fields = [load(first) for first in firsts]
    centres_of = [jnp.mean(field, axis=0, keepdims=True) for field in fields]
    fields = [field - centre for field, centre in zip(fields, centres_of)]
    for b in range(4):
        n = starts[b + 1] - starts[b]
        x = obs[starts[b] : starts[b + 1], :]
        member = lane_of((n, LANES)) < members
        fact = lambda i: x[:, members + i : members + i + 1]
        shift = jnp.sum(jnp.where(member, x, 0.0), axis=1, keepdims=True) / members
        anomaly = jnp.where(member, x - shift, 0.0)
        average = centre_ref[starts[b] : starts[b + 1], 0:1] + shift
        spread = jnp.sum(anomaly * anomaly, axis=1, keepdims=True) / (members - 1) + epsilon
        live = fact(LIVE)
        noise = jnp.where(live > 0.5, fact(VARIANCE), 1.0)
        share = 1.0 / (spread + noise)
        increment = spread * share * (fact(READING) - average) + (jnp.sqrt(noise * share) - 1.0) * anomaly
        increment = jnp.where(member, increment, 0.0)
        scaled = anomaly * (live / ((members - 1) * spread))
        inc_ref[0:n, :] = increment
        ano_ref[0:n, :] = scaled
        at = centres[b] + 16 * parity
        gain_lhs[b] = beside(*halves(ano_ref[pl.ds(at, 80), :]))
        near_ref[b] = obs[pl.ds(starts[b] + at, 80), :]
        board[...] = jnp.zeros_like(board)
        board[0:80, :] = inc_ref[pl.ds(at, 80), :]
        inc_lhs[b] = beside(*halves(board[...].T[0:80, :]))
        gap = jnp.abs(cols - near_ref[b, :, members + COLUMN : members + COLUMN + 1])
        gap = jnp.minimum(gap, width - gap)
        closeness[b] = 1.0 - gap * gap * scale
        if b < 3:
            y = obs[starts[b + 1] : total, :]
            m = total - starts[b + 1]
            covariance = product(jnp.where(lane_of((m, LANES)) < members, y, 0.0), scaled, ((1,), (1,)))
            row_gap = y[:, members + ROW : members + ROW + 1] - across[0:1, starts[b] : starts[b + 1]]
            col_gap = jnp.abs(y[:, members + COLUMN : members + COLUMN + 1] - across[1:2, starts[b] : starts[b + 1]])
            col_gap = jnp.minimum(col_gap, width - col_gap)
            remain = jnp.maximum(1.0 - (row_gap * row_gap + col_gap * col_gap) * scale, 0.0)
            weights = remain * remain * covariance
            obs[starts[b + 1] : total, :] = y + product(weights, increment, ((1,), (0,)))
        if b < 3:
            fields = [assimilate(field, b, first) for field, first in zip(fields, firsts)]
    copies = []
    for first, field, centre in zip(firsts, fields, centres_of):
        state = assimilate(field, 3, first) + centre
        for i in range(together * rows):
            t, r = first + i // rows, i % rows
            updated[(t * rows + r) * members : (t * rows + r + 1) * members, :] = state[:, i * LANES : (i + 1) * LANES]
        cols = slice(first * LANES, (first + together) * LANES)
        for e in range(members):
            for t in range(first, first + together):
                line = updated[pl.ds(t * rows * members + e, rows, stride=members), :]
                whole[e, :, t * LANES : (t + 1) * LANES] = line
        copies.append(pltpu.make_async_copy(whole.at[:, :, cols], out_ref.at[:, :, cols], sems.at[first // together]))
        copies[-1].start()
    for copy in copies:
        copy.wait()


def local(tracer, diffusion, sites, readings, variances, tally):
    own, rows, width = tracer.shape
    regions = lax.axis_size("region")
    batches, slots = sites.shape
    quarter_width = width // QUARTERS
    members = own * QUARTERS
    region = lax.axis_index("region")
    quarter = lax.axis_index("member")
    vmem = pl.BlockSpec(memory_space=pltpu.VMEM)
    smem = pl.BlockSpec(memory_space=pltpu.SMEM)
    limit = pltpu.CompilerParams(vmem_limit_bytes=32 * 1024 * 1024)
    line = jax.ShapeDtypeStruct((own, width), f32)
    place = jnp.stack([region % 2, quarter, region, region // 2 % RING]).astype(jnp.int32)
    top, bottom = pl.pallas_call(
        edges_kernel, out_shape=(line, line), in_specs=[vmem], out_specs=(vmem, vmem), compiler_params=limit, name="edges"
    )(tracer)
    above = lax.ppermute(bottom, "region", [(i, i + 1) for i in range(regions - 1)])
    below = lax.ppermute(top, "region", [(i + 1, i) for i in range(regions - 1)])
    partial, board = pl.pallas_call(
        step_kernel,
        out_shape=(
            jax.ShapeDtypeStruct((own * rows * width // LANES, LANES), f32),
            jax.ShapeDtypeStruct((LANES, LANES), f32),
        ),
        in_specs=[smem] * 3 + [vmem] * 5,
        out_specs=(vmem, vmem),
        compiler_params=limit,
        cost_estimate=pl.CostEstimate(flops=20_000_000, bytes_accessed=10_000_000, transcendentals=0),
        name="step",
    )(region[None].astype(jnp.int32), sites, tally, tracer, diffusion, sites, readings, variances)
    parcel = pl.pallas_call(
        parcel_kernel,
        out_shape=jax.ShapeDtypeStruct((slots, LANES), f32),
        in_specs=[smem] + [vmem] * 4,
        out_specs=vmem,
        scratch_shapes=[pltpu.VMEM(((2 * width // LANES + 1) * 24, LANES), f32), pltpu.VMEM((LANES, LANES), f32)],
        compiler_params=limit,
        name="parcel",
    )(sites, board, above, below, diffusion)
    parcel, partial = lax.optimization_barrier((parcel, partial))
    planes = regions // 2 // RING
    swap = []
    for z in range(planes):
        for y in range(RING):
            to = z + (1 if y >= RING // 2 else -1)
            if 0 <= to < planes:
                swap += [((z * RING + y) * 2 + p, (to * RING + RING - 1 - y) * 2 + p) for p in range(2)]
    other = lax.ppermute(parcel, "region", swap)
    size = own * rows * quarter_width // LANES
    stay, near, cross = pl.pallas_call(
        finish_kernel,
        out_shape=[jax.ShapeDtypeStruct((n * size, LANES), f32) for n in (1, 1, 2)],
        in_specs=[smem] + [vmem] * 4,
        out_specs=[vmem] * 3,
        compiler_params=limit,
        cost_estimate=pl.CostEstimate(flops=10_000_000_000, bytes_accessed=4_000_000, transcendentals=0),
        name="finish",
    )(place, partial, above, below, diffusion)
    crossed = lax.ppermute(cross, "member", [(m, m ^ 2) for m in range(QUARTERS)])
    other, _ = lax.optimization_barrier((other, stay))
    repeated = pl.pallas_call(
        repeat_kernel,
        out_shape=jax.ShapeDtypeStruct((RING, 2 * slots, LANES), f32),
        in_specs=[vmem] * 2,
        out_specs=vmem,
        compiler_params=limit,
        cost_estimate=pl.CostEstimate(flops=50_000_000_000, bytes_accessed=2_000_000, transcendentals=0),
        name="repeat",
    )(parcel, other)
    rings = [[(z * RING + y) * 2 + p for y in range(RING)] for z in range(planes) for p in range(2)]
    plane = lax.all_to_all(repeated, "region", 0, 0, axis_index_groups=rings)
    to_core = [(m, m ^ 1) for m in range(QUARTERS)]
    states = [stay, lax.ppermute(near, "member", to_core), crossed, lax.ppermute(crossed[size:], "member", to_core)]
    packed = pl.pallas_call(
        pack_kernel,
        out_shape=jax.ShapeDtypeStruct((2 * QUARTERS, 6 * slots, LANES), f32),
        in_specs=[smem, vmem],
        out_specs=vmem,
        compiler_params=limit,
        cost_estimate=pl.CostEstimate(flops=1_000_000, bytes_accessed=2_000_000, transcendentals=0),
        name="pack",
    )(place, plane)
    lines = [[2 * QUARTERS * g + i for i in range(2 * QUARTERS)] for g in range(regions // 2)]
    parcels = lax.all_to_all(packed, ("region", "member"), 0, 0, axis_index_groups=lines)
    block = 2 * slots
    total = 24 * block
    return pl.pallas_call(
        functools.partial(update_kernel, width=width),
        out_shape=jax.ShapeDtypeStruct((members, rows, quarter_width), f32),
        in_specs=[smem] + [vmem] * 5,
        out_specs=pl.BlockSpec(memory_space=pl.ANY),
        scratch_shapes=[
            pltpu.VMEM((total, LANES), f32),
            pltpu.VMEM((9 * block, LANES), f32),
            pltpu.VMEM((9 * block, LANES), f32),
            pltpu.VMEM((4, 80, 256), bf16),
            pltpu.VMEM((4, 80, 256), bf16),
            pltpu.VMEM((4, 80, LANES), f32),
            pltpu.VMEM((LANES, LANES), f32),
            pltpu.VMEM((members * rows * quarter_width // LANES, LANES), f32),
            pltpu.VMEM((members * rows * quarter_width // LANES, LANES), f32),
            pltpu.VMEM((members, rows, quarter_width), f32),
            pltpu.VMEM((total, LANES), f32),
            pltpu.SemaphoreType.DMA((2,)),
        ],
        compiler_params=limit,
        name="update",
    )(place, parcels, *states)


def solution(mesh):
    placed = (
        P("member", "region", None),
        P("region", None),
        P(None, "region"),
        P(None, "region"),
        P(None, "region"),
        P(),
    )
    return jax.shard_map(
        local, mesh=mesh, in_specs=placed, out_specs=P(None, "region", "member"), check_vma=False
    )
```

```python
import functools

import jax
import jax.numpy as jnp
from jax import lax
from jax.experimental import pallas as pl
from jax.experimental.pallas import tpu as pltpu
from jax.sharding import PartitionSpec as P

REACH = 2
RADIUS = 16
epsilon = 1e-05
LANES = 128
QUARTERS = 4
RING = 8
f32 = jnp.float32
bf16 = jnp.bfloat16

FACTS = 5
READING, VARIANCE, ROW, COLUMN, LIVE = range(FACTS)


def lane_of(shape):
    return lax.broadcasted_iota(jnp.int32, shape, len(shape) - 1)


def row_of(shape):
    return lax.broadcasted_iota(jnp.int32, shape, len(shape) - 2)


def halves(x):
    hi = x.astype(bf16).astype(f32)
    return hi, x - hi


def product(a, b, dims):
    a_hi, a_lo = [v.astype(bf16) for v in halves(a)]
    b_hi, b_lo = [v.astype(bf16) for v in halves(b)]
    dot = functools.partial(lax.dot_general, dimension_numbers=(dims, ((), ())), preferred_element_type=f32)
    return dot(a_hi, b_hi) + (dot(a_hi, b_lo) + dot(a_lo, b_hi))


def edges_kernel(tracer_ref, top_ref, bottom_ref):
    own, rows, _ = tracer_ref.shape
    for e in range(own):
        top_ref[e : e + 1, :] = tracer_ref[e, 0:1, :]
        bottom_ref[e : e + 1, :] = tracer_ref[e, rows - 1 : rows, :]


def step_kernel(
    region_ref, site_ref, tally_ref, tracer_ref, diffusion_ref, site_vec_ref, reading_ref, variance_ref,
    partial_ref, board_ref, spot_ref,
):
    own, rows, width = tracer_ref.shape
    batches, slots = site_ref.shape
    tiles = width // LANES // QUARTERS
    region = region_ref[0]
    diffusion = diffusion_ref[...]
    row = row_of((rows, width))
    for e in range(own):
        x = tracer_ref[e]
        lower = jnp.where(row == 0, 0.0, pltpu.roll(x, 1, 0))
        upper = jnp.where(row == rows - 1, 0.0, pltpu.roll(x, rows - 1, 0))
        east = pltpu.roll(x, width - 1, 1)
        west = pltpu.roll(x, 1, 1)
        y = x + diffusion * (upper + lower + east + west - 4.0 * x)
        for q in range(QUARTERS):
            for t in range(tiles):
                at = ((q * own + e) * tiles + t) * rows
                col = (q * tiles + t) * LANES
                partial_ref[at : at + rows, :] = y[:, col : col + LANES]
    board_ref[...] = jnp.zeros_like(board_ref)
    lane = lane_of((own, LANES))
    for b in range(batches):
        picked = jnp.zeros((own, LANES), f32)
        for k in range(slots):
            cell = site_ref[b, k]
            col = lax.rem(cell, width)
            tile = lax.div(col, LANES)
            start = lax.div(tile, tiles) * (own * tiles * rows) + lax.rem(tile, tiles) * rows + lax.div(cell, width)
            line = partial_ref[pl.ds(start, own, stride=tiles * rows), :]
            shift = lax.rem(k - lax.rem(col, LANES) + LANES, LANES)
            picked = jnp.where(lane == k, pltpu.roll(line, shift, 1), picked)
            row = lax.div(cell, width)
            block = jnp.where(row == 0, tile, jnp.where(row == rows - 1, QUARTERS * tiles + tile, 2 * QUARTERS * tiles))
            spot_ref[b, k] = block * 24
            spot_ref[batches + b, k] = shift
        at = b * 32
        board_ref[at : at + own, :] = picked
        cells = site_vec_ref[b : b + 1, :]
        count = tally_ref[b, region]
        facts = [
            reading_ref[b : b + 1, :],
            variance_ref[b : b + 1, :],
            (region * rows + lax.div(cells, width)).astype(f32),
            lax.rem(cells, width).astype(f32),
            jnp.where(lane_of((1, slots)) < count, 1.0, 0.0),
        ]
        for i, fact in enumerate(facts):
            board_ref[at + own + i : at + own + i + 1, 0:slots] = fact


def parcel_kernel(spot_ref, board_ref, above_ref, below_ref, diffusion_ref, parcel_ref, halo, board):
    own, width = above_ref.shape
    batches, slots = spot_ref.shape[0] // 2, spot_ref.shape[1]
    rows = diffusion_ref.shape[0]
    tiles = width // LANES
    for t in range(tiles):
        cols = slice(t * LANES, (t + 1) * LANES)
        halo[t * 24 : t * 24 + own, :] = above_ref[:, cols] * diffusion_ref[0:1, cols]
        halo[(tiles + t) * 24 : (tiles + t) * 24 + own, :] = below_ref[:, cols] * diffusion_ref[rows - 1 : rows, cols]
    halo[2 * tiles * 24 : 2 * tiles * 24 + 24, :] = jnp.zeros((24, LANES), f32)
    lane = lane_of((24, LANES))
    for b in range(batches):
        picked = jnp.zeros((24, LANES), f32)
        for k in range(slots):
            line = halo[pl.ds(pl.multiple_of(spot_ref[b, k], 8), 24), :]
            shift = spot_ref[batches + b, k]
            picked = jnp.where(lane == k, pltpu.roll(line, shift, 1), picked)
        picked = jnp.where(row_of((24, LANES)) < own, picked, 0.0)
        board[b * 32 : b * 32 + 24, :] = board_ref[b * 32 : b * 32 + 24, :] + picked
        board[b * 32 + 24 : b * 32 + 32, :] = board_ref[b * 32 + 24 : b * 32 + 32, :]
    parcel_ref[...] = board[...].T[:slots, :]


def repeat_kernel(own_ref, other_ref, out_ref):
    slots = own_ref.shape[0]
    for i in range(out_ref.shape[0]):
        out_ref[i, 0:slots, :] = own_ref[...]
        out_ref[i, slots : 2 * slots, :] = other_ref[...]


def finish_kernel(place_ref, partial_ref, above_ref, below_ref, diffusion_ref, stay_ref, near_ref, cross_ref):
    own = above_ref.shape[0]
    rows = diffusion_ref.shape[0]
    tiles = above_ref.shape[1] // LANES // QUARTERS
    size = own * tiles * rows
    row = row_of((rows, LANES))
    for i, (out_ref, base) in enumerate(((stay_ref, 0), (near_ref, 0), (cross_ref, 0), (cross_ref, size))):
        quarter = jnp.bitwise_xor(place_ref[1], i)
        for t in range(tiles):
            cols = pl.ds(pl.multiple_of((quarter * tiles + t) * LANES, LANES), LANES)
            diffusion = diffusion_ref[:, cols]
            first = jnp.where(row == 0, diffusion, 0.0)
            last = jnp.where(row == rows - 1, diffusion, 0.0)
            for e in range(own):
                at = (e * tiles + t) * rows
                part = partial_ref[pl.ds(pl.multiple_of(quarter * size + at, 8), rows), :]
                part = part + first * above_ref[e : e + 1, cols] + last * below_ref[e : e + 1, cols]
                out_ref[base + at : base + at + rows, :] = part


def pack_kernel(place_ref, plane_ref, out_ref):
    count = plane_ref.shape[0]
    slots = plane_ref.shape[1] // 2
    y = place_ref[3]

    def parcel(o):
        at = y + o
        inside = (at >= 0) & (at < count)
        at = lax.rem(at + count, count)
        return jnp.where(inside, plane_ref[at, 0:slots], plane_ref[count - 1 - at, slots : 2 * slots])

    lane = lane_of((slots, LANES))
    groups = [parcel(o) for o in (-1, 0, 1)]
    groups.append(jnp.where(lane < 96, parcel(-2), pltpu.roll(parcel(-4), 96, 1)))
    groups.append(jnp.where(lane < 96, parcel(2), pltpu.roll(parcel(4), 96, 1)))
    groups.append(jnp.where(lane < 64, parcel(-3), pltpu.roll(parcel(3), 64, 1)))
    for i in range(out_ref.shape[0]):
        for g, group in enumerate(groups):
            out_ref[i, g * slots : (g + 1) * slots, :] = group


def packed_at(offset, batch):
    if abs(offset) <= 1:
        return offset + 1, batch
    if abs(offset) == 3:
        return 5, batch + (2 if offset > 0 else 0)
    return (3 if offset < 0 else 4), (batch if abs(offset) == 2 else 3)


def beside(hi, lo):
    lane = lane_of(hi.shape)
    again = pltpu.roll(hi, 80, 1)
    last = pltpu.roll(lo, 32, 1)
    first = jnp.where(lane < 80, hi, again)
    second = jnp.where(lane < 32, again, last)
    return jnp.concatenate([first.astype(bf16), second.astype(bf16)], axis=1)


def below_each_other(x):
    hi, lo = halves(x)
    hi, lo = hi.astype(bf16), lo.astype(bf16)
    return jnp.concatenate([hi, lo, hi, jnp.zeros((16, x.shape[1]), bf16)], axis=0)


def update_kernel(
    place_ref, parcels_ref, state0_ref, state1_ref, state2_ref, state3_ref,
    out_ref, obs, inc_ref, ano_ref, gain_lhs, inc_lhs, near_ref, board, state_ref, updated, whole, centre_ref, sems, *, width,
):
    members = 80
    parity = place_ref[0]
    quarter = place_ref[1]
    region = place_ref[2]
    rows, quarter_width = out_ref.shape[1:]
    tiles = quarter_width // LANES
    scale = 1.0 / (RADIUS * RADIUS)
    own = members // QUARTERS
    slots = parcels_ref.shape[1] // 6
    lane = lane_of((slots, LANES))
    blocks = [(o, b) for b in range(4) for o in range(b - 4, 5 - b)]
    for i, (o, b) in enumerate(blocks):
        group, block = packed_at(o, b)
        for p in range(2):
            total = jnp.zeros((slots, LANES), f32)
            for m in range(QUARTERS):
                piece = parcels_ref[p * QUARTERS + m, group * slots : (group + 1) * slots, :]
                moved = pltpu.roll(piece, (own * m - 32 * block) % LANES, 1)
                end = own * (m + 1) + (FACTS if m == QUARTERS - 1 else 0)
                total = jnp.where((lane >= own * m) & (lane < end), moved, total)
            obs[(2 * i + p) * slots : (2 * i + p + 1) * slots, :] = total
    for i, ref in enumerate((state0_ref, state1_ref, state2_ref, state3_ref)):
        size = state0_ref.shape[0]
        at = pl.multiple_of(jnp.bitwise_xor(quarter, i) * size, 8)
        state_ref[pl.ds(at, size), :] = ref[0:size, :]
    starts = [0, 288, 512, 672, 768]
    centres = [96, 64, 32, 0]
    total = starts[-1]
    pick = jnp.where(lane_of((8, LANES)) == members + ROW + row_of((8, LANES)), 1.0, 0.0).astype(bf16)
    across = sum(
        lax.dot_general(pick, half.astype(bf16), (((1,), (1,)), ((), ())), preferred_element_type=f32)
        for half in halves(obs[...])
    )
    everything = obs[...]
    inside = lane_of(everything.shape) < members
    centre = jnp.sum(jnp.where(inside, everything, 0.0), axis=1, keepdims=True) / members
    centre_ref[...] = jnp.broadcast_to(centre, everything.shape)
    obs[...] = jnp.where(inside, everything - centre, everything)
    cols = (lane_of((80, quarter_width)) + quarter * quarter_width).astype(f32)
    closeness = {}
    together = 4

    def load(first):
        lines = [(r, t) for t in range(first, first + together) for r in range(rows)]
        return jnp.concatenate([state_ref[pl.ds(t * rows + r, members, stride=tiles * rows), :] for r, t in lines], axis=1)

    def assimilate(state, b, first):
        covariance = jnp.dot(gain_lhs[b], below_each_other(state), preferred_element_type=f32)
        tapers = []
        for t in range(first, first + together):
            near = closeness[b][:, t * LANES : (t + 1) * LANES]
            for r in range(rows):
                gap = (region * rows + r).astype(f32) - near_ref[b, :, members + ROW : members + ROW + 1]
                remain = jnp.maximum(near - gap * gap * scale, 0.0)
                tapers.append(remain * remain)
        weights = jnp.concatenate(tapers, axis=1) * covariance
        return state + jnp.dot(inc_lhs[b], below_each_other(weights), preferred_element_type=f32)

    firsts = range(0, tiles, together)
    fields = [load(first) for first in firsts]
    centres_of = [jnp.mean(field, axis=0, keepdims=True) for field in fields]
    fields = [field - centre for field, centre in zip(fields, centres_of)]
    for b in range(4):
        n = starts[b + 1] - starts[b]
        x = obs[starts[b] : starts[b + 1], :]
        member = lane_of((n, LANES)) < members
        fact = lambda i: x[:, members + i : members + i + 1]
        shift = jnp.sum(jnp.where(member, x, 0.0), axis=1, keepdims=True) / members
        anomaly = jnp.where(member, x - shift, 0.0)
        average = centre_ref[starts[b] : starts[b + 1], 0:1] + shift
        spread = jnp.sum(anomaly * anomaly, axis=1, keepdims=True) / (members - 1) + epsilon
        live = fact(LIVE)
        noise = jnp.where(live > 0.5, fact(VARIANCE), 1.0)
        share = 1.0 / (spread + noise)
        increment = spread * share * (fact(READING) - average) + (jnp.sqrt(noise * share) - 1.0) * anomaly
        increment = jnp.where(member, increment, 0.0)
        scaled = anomaly * (live / ((members - 1) * spread))
        inc_ref[0:n, :] = increment
        ano_ref[0:n, :] = scaled
        at = centres[b] + 16 * parity
        gain_lhs[b] = beside(*halves(ano_ref[pl.ds(at, 80), :]))
        near_ref[b] = obs[pl.ds(starts[b] + at, 80), :]
        board[...] = jnp.zeros_like(board)
        board[0:80, :] = inc_ref[pl.ds(at, 80), :]
        inc_lhs[b] = beside(*halves(board[...].T[0:80, :]))
        gap = jnp.abs(cols - near_ref[b, :, members + COLUMN : members + COLUMN + 1])
        gap = jnp.minimum(gap, width - gap)
        closeness[b] = 1.0 - gap * gap * scale
        if b < 3:
            y = obs[starts[b + 1] : total, :]
            m = total - starts[b + 1]
            covariance = product(jnp.where(lane_of((m, LANES)) < members, y, 0.0), scaled, ((1,), (1,)))
            row_gap = y[:, members + ROW : members + ROW + 1] - across[0:1, starts[b] : starts[b + 1]]
            col_gap = jnp.abs(y[:, members + COLUMN : members + COLUMN + 1] - across[1:2, starts[b] : starts[b + 1]])
            col_gap = jnp.minimum(col_gap, width - col_gap)
            remain = jnp.maximum(1.0 - (row_gap * row_gap + col_gap * col_gap) * scale, 0.0)
            weights = remain * remain * covariance
            obs[starts[b + 1] : total, :] = y + product(weights, increment, ((1,), (0,)))
        if b < 3:
            fields = [assimilate(field, b, first) for field, first in zip(fields, firsts)]
    state = assimilate(fields[0], 3, 0) + centres_of[0]
    copies = []
    for half in range(2):
        for t in range(half * tiles // 2, (half + 1) * tiles // 2):
            for r in range(rows):
                i = t * rows + r
                updated[i * members : (i + 1) * members, :] = state[:, i * LANES : (i + 1) * LANES]
            for e in range(members):
                line = updated[pl.ds(t * rows * members + e, rows, stride=members), :]
                whole[e, :, t * LANES : (t + 1) * LANES] = line
        cols = pl.ds(half * quarter_width // 2, quarter_width // 2)
        copies.append(pltpu.make_async_copy(whole.at[:, :, cols], out_ref.at[:, :, cols], sems.at[half]))
        copies[-1].start()
    for copy in copies:
        copy.wait()


def local(tracer, diffusion, sites, readings, variances, tally):
    own, rows, width = tracer.shape
    regions = lax.axis_size("region")
    batches, slots = sites.shape
    quarter_width = width // QUARTERS
    members = own * QUARTERS
    region = lax.axis_index("region")
    quarter = lax.axis_index("member")
    vmem = pl.BlockSpec(memory_space=pltpu.VMEM)
    smem = pl.BlockSpec(memory_space=pltpu.SMEM)
    limit = pltpu.CompilerParams(vmem_limit_bytes=32 * 1024 * 1024)
    line = jax.ShapeDtypeStruct((own, width), f32)
    place = jnp.stack([region % 2, quarter, region, region // 2 % RING]).astype(jnp.int32)
    top, bottom = pl.pallas_call(
        edges_kernel, out_shape=(line, line), in_specs=[vmem], out_specs=(vmem, vmem), compiler_params=limit, name="edges"
    )(tracer)
    above = lax.ppermute(bottom, "region", [(i, i + 1) for i in range(regions - 1)])
    below = lax.ppermute(top, "region", [(i + 1, i) for i in range(regions - 1)])
    partial, board, spots = pl.pallas_call(
        step_kernel,
        out_shape=(
            jax.ShapeDtypeStruct((own * rows * width // LANES, LANES), f32),
            jax.ShapeDtypeStruct((LANES, LANES), f32),
            jax.ShapeDtypeStruct((2 * batches, slots), jnp.int32),
        ),
        in_specs=[smem] * 3 + [vmem] * 5,
        out_specs=(vmem, vmem, smem),
        compiler_params=limit,
        cost_estimate=pl.CostEstimate(flops=20_000_000, bytes_accessed=10_000_000, transcendentals=0),
        name="step",
    )(region[None].astype(jnp.int32), sites, tally, tracer, diffusion, sites, readings, variances)
    parcel = pl.pallas_call(
        parcel_kernel,
        out_shape=jax.ShapeDtypeStruct((slots, LANES), f32),
        in_specs=[smem] + [vmem] * 4,
        out_specs=vmem,
        scratch_shapes=[pltpu.VMEM(((2 * width // LANES + 1) * 24, LANES), f32), pltpu.VMEM((LANES, LANES), f32)],
        compiler_params=limit,
        name="parcel",
    )(spots, board, above, below, diffusion)
    parcel, partial = lax.optimization_barrier((parcel, partial))
    planes = regions // 2 // RING
    swap = []
    for z in range(planes):
        for y in range(RING):
            to = z + (1 if y >= RING // 2 else -1)
            if 0 <= to < planes:
                swap += [((z * RING + y) * 2 + p, (to * RING + RING - 1 - y) * 2 + p) for p in range(2)]
    other = lax.ppermute(parcel, "region", swap)
    size = own * rows * quarter_width // LANES
    stay, near, cross = pl.pallas_call(
        finish_kernel,
        out_shape=[jax.ShapeDtypeStruct((n * size, LANES), f32) for n in (1, 1, 2)],
        in_specs=[smem] + [vmem] * 4,
        out_specs=[vmem] * 3,
        compiler_params=limit,
        cost_estimate=pl.CostEstimate(flops=10_000_000_000, bytes_accessed=4_000_000, transcendentals=0),
        name="finish",
    )(place, partial, above, below, diffusion)
    crossed = lax.ppermute(cross, "member", [(m, m ^ 2) for m in range(QUARTERS)])
    other, _ = lax.optimization_barrier((other, stay))
    repeated = pl.pallas_call(
        repeat_kernel,
        out_shape=jax.ShapeDtypeStruct((RING, 2 * slots, LANES), f32),
        in_specs=[vmem] * 2,
        out_specs=vmem,
        compiler_params=limit,
        cost_estimate=pl.CostEstimate(flops=50_000_000_000, bytes_accessed=2_000_000, transcendentals=0),
        name="repeat",
    )(parcel, other)
    rings = [[(z * RING + y) * 2 + p for y in range(RING)] for z in range(planes) for p in range(2)]
    plane = lax.all_to_all(repeated, "region", 0, 0, axis_index_groups=rings)
    to_core = [(m, m ^ 1) for m in range(QUARTERS)]
    states = [stay, lax.ppermute(near, "member", to_core), crossed, lax.ppermute(crossed[size:], "member", to_core)]
    packed = pl.pallas_call(
        pack_kernel,
        out_shape=jax.ShapeDtypeStruct((2 * QUARTERS, 6 * slots, LANES), f32),
        in_specs=[smem, vmem],
        out_specs=vmem,
        compiler_params=limit,
        cost_estimate=pl.CostEstimate(flops=1_000_000, bytes_accessed=2_000_000, transcendentals=0),
        name="pack",
    )(place, plane)
    lines = [[2 * QUARTERS * g + i for i in range(2 * QUARTERS)] for g in range(regions // 2)]
    parcels = lax.all_to_all(packed, ("region", "member"), 0, 0, axis_index_groups=lines)
    block = 2 * slots
    total = 24 * block
    return pl.pallas_call(
        functools.partial(update_kernel, width=width),
        out_shape=jax.ShapeDtypeStruct((members, rows, quarter_width), f32),
        in_specs=[smem] + [vmem] * 5,
        out_specs=pl.BlockSpec(memory_space=pl.ANY),
        scratch_shapes=[
            pltpu.VMEM((total, LANES), f32),
            pltpu.VMEM((9 * block, LANES), f32),
            pltpu.VMEM((9 * block, LANES), f32),
            pltpu.VMEM((4, 80, 256), bf16),
            pltpu.VMEM((4, 80, 256), bf16),
            pltpu.VMEM((4, 80, LANES), f32),
            pltpu.VMEM((LANES, LANES), f32),
            pltpu.VMEM((members * rows * quarter_width // LANES, LANES), f32),
            pltpu.VMEM((members * rows * quarter_width // LANES, LANES), f32),
            pltpu.VMEM((members, rows, quarter_width), f32),
            pltpu.VMEM((total, LANES), f32),
            pltpu.SemaphoreType.DMA((2,)),
        ],
        compiler_params=limit,
        name="update",
    )(place, parcels, *states)


def solution(mesh):
    placed = (
        P("member", "region", None),
        P("region", None),
        P(None, "region"),
        P(None, "region"),
        P(None, "region"),
        P(),
    )
    return jax.shard_map(
        local, mesh=mesh, in_specs=placed, out_specs=P(None, "region", "member"), check_vma=False
    )
```

```python
import functools

import jax
import jax.numpy as jnp
from jax import lax
from jax.experimental import pallas as pl
from jax.experimental.pallas import tpu as pltpu
from jax.sharding import PartitionSpec as P

REACH = 2
RADIUS = 16
epsilon = 1e-05
LANES = 128
QUARTERS = 4
RING = 8
f32 = jnp.float32
bf16 = jnp.bfloat16

FACTS = 5
READING, VARIANCE, ROW, COLUMN, LIVE = range(FACTS)


def lane_of(shape):
    return lax.broadcasted_iota(jnp.int32, shape, len(shape) - 1)


def row_of(shape):
    return lax.broadcasted_iota(jnp.int32, shape, len(shape) - 2)


def halves(x):
    hi = x.astype(bf16).astype(f32)
    return hi, x - hi


def product(a, b, dims):
    a_hi, a_lo = [v.astype(bf16) for v in halves(a)]
    b_hi, b_lo = [v.astype(bf16) for v in halves(b)]
    dot = functools.partial(lax.dot_general, dimension_numbers=(dims, ((), ())), preferred_element_type=f32)
    return dot(a_hi, b_hi) + (dot(a_hi, b_lo) + dot(a_lo, b_hi))


def edges_kernel(tracer_ref, top_ref, bottom_ref):
    own, rows, _ = tracer_ref.shape
    for e in range(own):
        top_ref[e : e + 1, :] = tracer_ref[e, 0:1, :]
        bottom_ref[e : e + 1, :] = tracer_ref[e, rows - 1 : rows, :]


def step_kernel(
    region_ref, site_ref, tally_ref, tracer_ref, diffusion_ref, site_vec_ref, reading_ref, variance_ref,
    partial_ref, board_ref, spot_ref,
):
    own, rows, width = tracer_ref.shape
    batches, slots = site_ref.shape
    tiles = width // LANES // QUARTERS
    region = region_ref[0]
    diffusion = diffusion_ref[...]
    row = row_of((rows, width))
    for e in range(own):
        x = tracer_ref[e]
        lower = jnp.where(row == 0, 0.0, pltpu.roll(x, 1, 0))
        upper = jnp.where(row == rows - 1, 0.0, pltpu.roll(x, rows - 1, 0))
        east = pltpu.roll(x, width - 1, 1)
        west = pltpu.roll(x, 1, 1)
        y = x + diffusion * (upper + lower + east + west - 4.0 * x)
        for q in range(QUARTERS):
            for t in range(tiles):
                at = ((q * own + e) * tiles + t) * rows
                col = (q * tiles + t) * LANES
                partial_ref[at : at + rows, :] = y[:, col : col + LANES]
    board_ref[...] = jnp.zeros_like(board_ref)
    lane = lane_of((own, LANES))
    for b in range(batches):
        picked = jnp.zeros((own, LANES), f32)
        for k in range(slots):
            cell = site_ref[b, k]
            col = lax.rem(cell, width)
            tile = lax.div(col, LANES)
            start = lax.div(tile, tiles) * (own * tiles * rows) + lax.rem(tile, tiles) * rows + lax.div(cell, width)
            line = partial_ref[pl.ds(start, own, stride=tiles * rows), :]
            shift = lax.rem(k - lax.rem(col, LANES) + LANES, LANES)
            picked = jnp.where(lane == k, pltpu.roll(line, shift, 1), picked)
            row = lax.div(cell, width)
            block = jnp.where(row == 0, tile, jnp.where(row == rows - 1, QUARTERS * tiles + tile, 2 * QUARTERS * tiles))
            spot_ref[b, k] = block * 24
            spot_ref[batches + b, k] = shift
        at = b * 32
        board_ref[at : at + own, :] = picked
        cells = site_vec_ref[b : b + 1, :]
        count = tally_ref[b, region]
        facts = [
            reading_ref[b : b + 1, :],
            variance_ref[b : b + 1, :],
            (region * rows + lax.div(cells, width)).astype(f32),
            lax.rem(cells, width).astype(f32),
            jnp.where(lane_of((1, slots)) < count, 1.0, 0.0),
        ]
        for i, fact in enumerate(facts):
            board_ref[at + own + i : at + own + i + 1, 0:slots] = fact


def parcel_kernel(spot_ref, board_ref, above_ref, below_ref, diffusion_ref, parcel_ref, halo, board):
    own, width = above_ref.shape
    batches, slots = spot_ref.shape[0] // 2, spot_ref.shape[1]
    rows = diffusion_ref.shape[0]
    tiles = width // LANES
    for t in range(tiles):
        cols = slice(t * LANES, (t + 1) * LANES)
        halo[t * 24 : t * 24 + own, :] = above_ref[:, cols] * diffusion_ref[0:1, cols]
        halo[(tiles + t) * 24 : (tiles + t) * 24 + own, :] = below_ref[:, cols] * diffusion_ref[rows - 1 : rows, cols]
    halo[2 * tiles * 24 : 2 * tiles * 24 + 24, :] = jnp.zeros((24, LANES), f32)
    lane = lane_of((24, LANES))
    for b in range(batches):
        picked = jnp.zeros((24, LANES), f32)
        for k in range(slots):
            line = halo[pl.ds(pl.multiple_of(spot_ref[b, k], 8), 24), :]
            shift = spot_ref[batches + b, k]
            picked = jnp.where(lane == k, pltpu.roll(line, shift, 1), picked)
        picked = jnp.where(row_of((24, LANES)) < own, picked, 0.0)
        board[b * 32 : b * 32 + 24, :] = board_ref[b * 32 : b * 32 + 24, :] + picked
        board[b * 32 + 24 : b * 32 + 32, :] = board_ref[b * 32 + 24 : b * 32 + 32, :]
    parcel_ref[...] = board[...].T[:slots, :]


def repeat_kernel(own_ref, other_ref, out_ref):
    slots = own_ref.shape[0]
    for i in range(out_ref.shape[0]):
        out_ref[i, 0:slots, :] = own_ref[...]
        out_ref[i, slots : 2 * slots, :] = other_ref[...]


def finish_kernel(place_ref, partial_ref, above_ref, below_ref, diffusion_ref, stay_ref, near_ref, cross_ref):
    own = above_ref.shape[0]
    rows = diffusion_ref.shape[0]
    tiles = above_ref.shape[1] // LANES // QUARTERS
    size = own * tiles * rows
    row = row_of((rows, LANES))
    for i, (out_ref, base) in enumerate(((stay_ref, 0), (near_ref, 0), (cross_ref, 0), (cross_ref, size))):
        quarter = jnp.bitwise_xor(place_ref[1], i)
        for t in range(tiles):
            cols = pl.ds(pl.multiple_of((quarter * tiles + t) * LANES, LANES), LANES)
            diffusion = diffusion_ref[:, cols]
            first = jnp.where(row == 0, diffusion, 0.0)
            last = jnp.where(row == rows - 1, diffusion, 0.0)
            for e in range(own):
                at = (e * tiles + t) * rows
                part = partial_ref[pl.ds(pl.multiple_of(quarter * size + at, 8), rows), :]
                part = part + first * above_ref[e : e + 1, cols] + last * below_ref[e : e + 1, cols]
                out_ref[base + at : base + at + rows, :] = part


def pack_kernel(place_ref, plane_ref, out_ref, packed, sems):
    count = plane_ref.shape[0]
    slots = plane_ref.shape[1] // 2
    y = place_ref[3]

    def parcel(o):
        at = y + o
        inside = (at >= 0) & (at < count)
        at = lax.rem(at + count, count)
        return jnp.where(inside, plane_ref[at, 0:slots], plane_ref[count - 1 - at, slots : 2 * slots])

    lane = lane_of((slots, LANES))
    groups = [parcel(o) for o in (-1, 0, 1)]
    groups.append(jnp.where(lane < 96, parcel(-2), pltpu.roll(parcel(-4), 96, 1)))
    groups.append(jnp.where(lane < 96, parcel(2), pltpu.roll(parcel(4), 96, 1)))
    groups.append(jnp.where(lane < 64, parcel(-3), pltpu.roll(parcel(3), 64, 1)))
    for g, group in enumerate(groups):
        packed[g * slots : (g + 1) * slots, :] = group
    copies = [pltpu.make_async_copy(packed, out_ref.at[i], sems.at[i]) for i in range(out_ref.shape[0])]
    for copy in copies:
        copy.start()
    for copy in copies:
        copy.wait()


def packed_at(offset, batch):
    if abs(offset) <= 1:
        return offset + 1, batch
    if abs(offset) == 3:
        return 5, batch + (2 if offset > 0 else 0)
    return (3 if offset < 0 else 4), (batch if abs(offset) == 2 else 3)


def beside(hi, lo):
    lane = lane_of(hi.shape)
    again = pltpu.roll(hi, 80, 1)
    last = pltpu.roll(lo, 32, 1)
    first = jnp.where(lane < 80, hi, again)
    second = jnp.where(lane < 32, again, last)
    return jnp.concatenate([first.astype(bf16), second.astype(bf16)], axis=1)


def below_each_other(x):
    hi, lo = halves(x)
    hi, lo = hi.astype(bf16), lo.astype(bf16)
    return jnp.concatenate([hi, lo, hi, jnp.zeros((16, x.shape[1]), bf16)], axis=0)


def update_kernel(
    place_ref, parcels_ref, state0_ref, state1_ref, state2_ref, state3_ref,
    out_ref, obs, inc_ref, ano_ref, gain_lhs, inc_lhs, near_ref, board, state_ref, updated, whole, centre_ref, sems, *, width,
):
    members = 80
    parity = place_ref[0]
    quarter = place_ref[1]
    region = place_ref[2]
    rows, quarter_width = out_ref.shape[1:]
    tiles = quarter_width // LANES
    scale = 1.0 / (RADIUS * RADIUS)
    own = members // QUARTERS
    slots = parcels_ref.shape[1] // 6
    lane = lane_of((slots, LANES))
    blocks = [(o, b) for b in range(4) for o in range(b - 4, 5 - b)]
    for i, (o, b) in enumerate(blocks):
        group, block = packed_at(o, b)
        for p in range(2):
            total = jnp.zeros((slots, LANES), f32)
            for m in range(QUARTERS):
                piece = parcels_ref[p * QUARTERS + m, group * slots : (group + 1) * slots, :]
                moved = pltpu.roll(piece, (own * m - 32 * block) % LANES, 1)
                end = own * (m + 1) + (FACTS if m == QUARTERS - 1 else 0)
                total = jnp.where((lane >= own * m) & (lane < end), moved, total)
            obs[(2 * i + p) * slots : (2 * i + p + 1) * slots, :] = total
    for i, ref in enumerate((state0_ref, state1_ref, state2_ref, state3_ref)):
        size = state0_ref.shape[0]
        at = pl.multiple_of(jnp.bitwise_xor(quarter, i) * size, 8)
        state_ref[pl.ds(at, size), :] = ref[0:size, :]
    starts = [0, 288, 512, 672, 768]
    centres = [96, 64, 32, 0]
    total = starts[-1]
    pick = jnp.where(lane_of((8, LANES)) == members + ROW + row_of((8, LANES)), 1.0, 0.0).astype(bf16)
    across = sum(
        lax.dot_general(pick, half.astype(bf16), (((1,), (1,)), ((), ())), preferred_element_type=f32)
        for half in halves(obs[...])
    )
    everything = obs[...]
    inside = lane_of(everything.shape) < members
    centre = jnp.sum(jnp.where(inside, everything, 0.0), axis=1, keepdims=True) / members
    centre_ref[...] = jnp.broadcast_to(centre, everything.shape)
    obs[...] = jnp.where(inside, everything - centre, everything)
    cols = (lane_of((80, quarter_width)) + quarter * quarter_width).astype(f32)
    closeness = {}
    together = 4

    def load(first):
        lines = [(r, t) for t in range(first, first + together) for r in range(rows)]
        return jnp.concatenate([state_ref[pl.ds(t * rows + r, members, stride=tiles * rows), :] for r, t in lines], axis=1)

    def assimilate(state, b, first):
        covariance = jnp.dot(gain_lhs[b], below_each_other(state), preferred_element_type=f32)
        tapers = []
        for t in range(first, first + together):
            near = closeness[b][:, t * LANES : (t + 1) * LANES]
            for r in range(rows):
                gap = (region * rows + r).astype(f32) - near_ref[b, :, members + ROW : members + ROW + 1]
                remain = jnp.maximum(near - gap * gap * scale, 0.0)
                tapers.append(remain * remain)
        weights = jnp.concatenate(tapers, axis=1) * covariance
        return state + jnp.dot(inc_lhs[b], below_each_other(weights), preferred_element_type=f32)

    firsts = range(0, tiles, together)
    fields = [load(first) for first in firsts]
    centres_of = [jnp.mean(field, axis=0, keepdims=True) for field in fields]
    fields = [field - centre for field, centre in zip(fields, centres_of)]
    for b in range(4):
        n = starts[b + 1] - starts[b]
        x = obs[starts[b] : starts[b + 1], :]
        member = lane_of((n, LANES)) < members
        fact = lambda i: x[:, members + i : members + i + 1]
        shift = jnp.sum(jnp.where(member, x, 0.0), axis=1, keepdims=True) / members
        anomaly = jnp.where(member, x - shift, 0.0)
        average = centre_ref[starts[b] : starts[b + 1], 0:1] + shift
        spread = jnp.sum(anomaly * anomaly, axis=1, keepdims=True) / (members - 1) + epsilon
        live = fact(LIVE)
        noise = jnp.where(live > 0.5, fact(VARIANCE), 1.0)
        share = 1.0 / (spread + noise)
        increment = spread * share * (fact(READING) - average) + (jnp.sqrt(noise * share) - 1.0) * anomaly
        increment = jnp.where(member, increment, 0.0)
        scaled = anomaly * (live / ((members - 1) * spread))
        inc_ref[0:n, :] = increment
        ano_ref[0:n, :] = scaled
        at = centres[b] + 16 * parity
        gain_lhs[b] = beside(*halves(ano_ref[pl.ds(at, 80), :]))
        near_ref[b] = obs[pl.ds(starts[b] + at, 80), :]
        board[...] = jnp.zeros_like(board)
        board[0:80, :] = inc_ref[pl.ds(at, 80), :]
        inc_lhs[b] = beside(*halves(board[...].T[0:80, :]))
        gap = jnp.abs(cols - near_ref[b, :, members + COLUMN : members + COLUMN + 1])
        gap = jnp.minimum(gap, width - gap)
        closeness[b] = 1.0 - gap * gap * scale
        if b < 3:
            y = obs[starts[b + 1] : total, :]
            m = total - starts[b + 1]
            covariance = product(jnp.where(lane_of((m, LANES)) < members, y, 0.0), scaled, ((1,), (1,)))
            row_gap = y[:, members + ROW : members + ROW + 1] - across[0:1, starts[b] : starts[b + 1]]
            col_gap = jnp.abs(y[:, members + COLUMN : members + COLUMN + 1] - across[1:2, starts[b] : starts[b + 1]])
            col_gap = jnp.minimum(col_gap, width - col_gap)
            remain = jnp.maximum(1.0 - (row_gap * row_gap + col_gap * col_gap) * scale, 0.0)
            weights = remain * remain * covariance
            obs[starts[b + 1] : total, :] = y + product(weights, increment, ((1,), (0,)))
        if b < 3:
            fields = [assimilate(field, b, first) for field, first in zip(fields, firsts)]
    state = assimilate(fields[0], 3, 0) + centres_of[0]
    copies = []
    for half in range(2):
        for t in range(half * tiles // 2, (half + 1) * tiles // 2):
            for r in range(rows):
                i = t * rows + r
                updated[i * members : (i + 1) * members, :] = state[:, i * LANES : (i + 1) * LANES]
            for e in range(members):
                line = updated[pl.ds(t * rows * members + e, rows, stride=members), :]
                whole[e, :, t * LANES : (t + 1) * LANES] = line
        cols = pl.ds(half * quarter_width // 2, quarter_width // 2)
        copies.append(pltpu.make_async_copy(whole.at[:, :, cols], out_ref.at[:, :, cols], sems.at[half]))
        copies[-1].start()
    for copy in copies:
        copy.wait()


def local(tracer, diffusion, sites, readings, variances, tally):
    own, rows, width = tracer.shape
    regions = lax.axis_size("region")
    batches, slots = sites.shape
    quarter_width = width // QUARTERS
    members = own * QUARTERS
    region = lax.axis_index("region")
    quarter = lax.axis_index("member")
    vmem = pl.BlockSpec(memory_space=pltpu.VMEM)
    smem = pl.BlockSpec(memory_space=pltpu.SMEM)
    limit = pltpu.CompilerParams(vmem_limit_bytes=32 * 1024 * 1024)
    line = jax.ShapeDtypeStruct((own, width), f32)
    place = jnp.stack([region % 2, quarter, region, region // 2 % RING]).astype(jnp.int32)
    top, bottom = pl.pallas_call(
        edges_kernel, out_shape=(line, line), in_specs=[vmem], out_specs=(vmem, vmem), compiler_params=limit, name="edges"
    )(tracer)
    above = lax.ppermute(bottom, "region", [(i, i + 1) for i in range(regions - 1)])
    below = lax.ppermute(top, "region", [(i + 1, i) for i in range(regions - 1)])
    partial, board, spots = pl.pallas_call(
        step_kernel,
        out_shape=(
            jax.ShapeDtypeStruct((own * rows * width // LANES, LANES), f32),
            jax.ShapeDtypeStruct((LANES, LANES), f32),
            jax.ShapeDtypeStruct((2 * batches, slots), jnp.int32),
        ),
        in_specs=[smem] * 3 + [vmem] * 5,
        out_specs=(vmem, vmem, smem),
        compiler_params=limit,
        cost_estimate=pl.CostEstimate(flops=20_000_000, bytes_accessed=10_000_000, transcendentals=0),
        name="step",
    )(region[None].astype(jnp.int32), sites, tally, tracer, diffusion, sites, readings, variances)
    parcel = pl.pallas_call(
        parcel_kernel,
        out_shape=jax.ShapeDtypeStruct((slots, LANES), f32),
        in_specs=[smem] + [vmem] * 4,
        out_specs=vmem,
        scratch_shapes=[pltpu.VMEM(((2 * width // LANES + 1) * 24, LANES), f32), pltpu.VMEM((LANES, LANES), f32)],
        compiler_params=limit,
        name="parcel",
    )(spots, board, above, below, diffusion)
    parcel, partial = lax.optimization_barrier((parcel, partial))
    planes = regions // 2 // RING
    swap = []
    for z in range(planes):
        for y in range(RING):
            to = z + (1 if y >= RING // 2 else -1)
            if 0 <= to < planes:
                swap += [((z * RING + y) * 2 + p, (to * RING + RING - 1 - y) * 2 + p) for p in range(2)]
    other = lax.ppermute(parcel, "region", swap)
    size = own * rows * quarter_width // LANES
    stay, near, cross = pl.pallas_call(
        finish_kernel,
        out_shape=[jax.ShapeDtypeStruct((n * size, LANES), f32) for n in (1, 1, 2)],
        in_specs=[smem] + [vmem] * 4,
        out_specs=[vmem] * 3,
        compiler_params=limit,
        cost_estimate=pl.CostEstimate(flops=10_000_000_000, bytes_accessed=4_000_000, transcendentals=0),
        name="finish",
    )(place, partial, above, below, diffusion)
    crossed = lax.ppermute(cross, "member", [(m, m ^ 2) for m in range(QUARTERS)])
    other, _ = lax.optimization_barrier((other, stay))
    repeated = pl.pallas_call(
        repeat_kernel,
        out_shape=jax.ShapeDtypeStruct((RING, 2 * slots, LANES), f32),
        in_specs=[vmem] * 2,
        out_specs=vmem,
        compiler_params=limit,
        cost_estimate=pl.CostEstimate(flops=50_000_000_000, bytes_accessed=2_000_000, transcendentals=0),
        name="repeat",
    )(parcel, other)
    rings = [[(z * RING + y) * 2 + p for y in range(RING)] for z in range(planes) for p in range(2)]
    plane = lax.all_to_all(repeated, "region", 0, 0, axis_index_groups=rings)
    to_core = [(m, m ^ 1) for m in range(QUARTERS)]
    states = [stay, lax.ppermute(near, "member", to_core), crossed, lax.ppermute(crossed[size:], "member", to_core)]
    packed = pl.pallas_call(
        pack_kernel,
        out_shape=jax.ShapeDtypeStruct((2 * QUARTERS, 6 * slots, LANES), f32),
        in_specs=[smem, vmem],
        out_specs=pl.BlockSpec(memory_space=pl.ANY),
        scratch_shapes=[pltpu.VMEM((6 * slots, LANES), f32), pltpu.SemaphoreType.DMA((2 * QUARTERS,))],
        compiler_params=limit,
        cost_estimate=pl.CostEstimate(flops=1_000_000, bytes_accessed=2_000_000, transcendentals=0),
        name="pack",
    )(place, plane)
    lines = [[2 * QUARTERS * g + i for i in range(2 * QUARTERS)] for g in range(regions // 2)]
    parcels = lax.all_to_all(packed, ("region", "member"), 0, 0, axis_index_groups=lines)
    block = 2 * slots
    total = 24 * block
    return pl.pallas_call(
        functools.partial(update_kernel, width=width),
        out_shape=jax.ShapeDtypeStruct((members, rows, quarter_width), f32),
        in_specs=[smem] + [vmem] * 5,
        out_specs=pl.BlockSpec(memory_space=pl.ANY),
        scratch_shapes=[
            pltpu.VMEM((total, LANES), f32),
            pltpu.VMEM((9 * block, LANES), f32),
            pltpu.VMEM((9 * block, LANES), f32),
            pltpu.VMEM((4, 80, 256), bf16),
            pltpu.VMEM((4, 80, 256), bf16),
            pltpu.VMEM((4, 80, LANES), f32),
            pltpu.VMEM((LANES, LANES), f32),
            pltpu.VMEM((members * rows * quarter_width // LANES, LANES), f32),
            pltpu.VMEM((members * rows * quarter_width // LANES, LANES), f32),
            pltpu.VMEM((members, rows, quarter_width), f32),
            pltpu.VMEM((total, LANES), f32),
            pltpu.SemaphoreType.DMA((2,)),
        ],
        compiler_params=limit,
        name="update",
    )(place, parcels, *states)


def solution(mesh):
    placed = (
        P("member", "region", None),
        P("region", None),
        P(None, "region"),
        P(None, "region"),
        P(None, "region"),
        P(),
    )
    return jax.shard_map(
        local, mesh=mesh, in_specs=placed, out_specs=P(None, "region", "member"), check_vma=False
    )
```
